256 devices in a mesh: space: 64 (over z, y, core), halo: 4 (over x).
Axes of the slice: x: 4, y: 4, z: 8, core: 2. Of those that a mesh axis runs over, the one named last changes fastest.
Arguments:
- positions: float32 [3, 1048576], P(None, 'space'), may hold values from -1 to 1
- masses: float32 [1048576], P('space'), may hold values from 0.1 to 10
- centres: float32 [4, 3, 1024], P('halo'), may hold values from -0.5 to 0.5
- pair_halo: int32 [4, 16384], P('halo', 'space'), may hold values from 0 to 1023
- pair_tile: int32 [4, 16384], P('halo', 'space'), may hold values from 0 to 31
- halo_slot: int32 [4, 1024], P('halo'), may hold values from 0 to 1023, each once within a row
- feedback: float32 [4, 1024], P('halo', 'space'), may hold values from 0.5 to 1.5
- mixing: float32 [3, 128, 128], replicated, may hold values from -0.5 to 0.5
- drive: float32 [3, 128], replicated, may hold values from 0.2 to 1
- readout: float32 [3, 128], replicated, may hold values from -1.5 to 1.5
Outputs:
- displacement: float32 [3, 1048576], P(None, 'space')
The draws below stay inside these ranges and needn't reach their ends.
All inputs are finite; a program needn't handle non-finite values.
Results may differ from the reference program's by a relative error of at most 0.0003.
Values sent between devices are 32-bit elements; how exact they have to be, the bound alone decides.
A program may use at most 64 MiB of HBM per device.

```python
import math
import jax
import jax.numpy as jnp
from jax import lax

K = 128
BLK = 512
ITERS = 8
PAIRS_DEV = 256
TILES_DEV = 32
HALOS_PER_GROUP = 1024
PAIRS = 16384
PARTICLES = 1048576
N_SPACE = 64
N_HALO = 4


def set_ends(result, own_key, smallest, top_value):
    longest = result.shape.index(max(result.shape))
    spots = []
    for shift in (0, 1):
        where = [jax.random.randint(jax.random.fold_in(own_key, axis), (), 0, length) for axis, length in enumerate(result.shape)]
        where[longest] = (where[longest] + shift) % result.shape[longest]
        spots.append(tuple(where))
    return result.at[spots[0]].set(smallest).at[spots[1]].set(top_value)


def level_of(rng, shape, split, smallest, high):
    factor_of, own = 1.0, jax.random.fold_in(rng, 6)
    for axis_at, parts in split:
        draws = jnp.exp(jax.random.uniform(jax.random.fold_in(own, axis_at), (parts,), jnp.float32, smallest / len(split), high / len(split)))
        factor_of = factor_of * jnp.repeat(draws, shape[axis_at] // parts).reshape([-1 if axis == axis_at else 1 for axis in range(len(shape))])
    return factor_of


def gaussian(stream_key, shape, width, most, held_as=jnp.bfloat16):
    result = width * jax.random.normal(stream_key, shape, jnp.float32)
    return jnp.clip(result, min=-most, max=most).astype(held_as)


def setup_inputs(seed: int = 0) -> dict:
    streams_of = jax.random.split(jax.random.key(seed), 11)
    positions = jnp.clip(jax.random.uniform(streams_of[0], (3, PARTICLES), jnp.float32, -1.0, 1.0) * level_of(streams_of[0], (3, PARTICLES), ((1, 64),), -0.4, 0.0), -1.0, 1.0)
    masses = jnp.clip(jnp.exp(math.log(10.0) - 4.6051702 * jax.random.uniform(streams_of[1], (PARTICLES,), jnp.float32) ** level_of(streams_of[1], (PARTICLES,), ((0, 64),), -0.2, 0.2)), 0.1, 10.0)
    centres = jnp.clip(jax.random.uniform(streams_of[2], (N_HALO, 3, HALOS_PER_GROUP), jnp.float32, -0.5, 0.5) * level_of(streams_of[2], (N_HALO, 3, HALOS_PER_GROUP), ((0, 4),), -0.4, 0.0), -0.5, 0.5)
    pair_halo = set_ends(jax.random.randint(streams_of[3], (N_HALO, PAIRS), 0, HALOS_PER_GROUP), jax.random.fold_in(streams_of[3], 1), 0, HALOS_PER_GROUP - 1).astype(jnp.int32)
    pair_tile = set_ends(jax.random.randint(streams_of[4], (N_HALO, PAIRS), 0, TILES_DEV), jax.random.fold_in(streams_of[4], 1), 0, TILES_DEV - 1).astype(jnp.int32)
    halo_slot = jax.vmap(lambda own: jax.random.permutation(own, HALOS_PER_GROUP))(jax.random.split(streams_of[5], N_HALO)).reshape((N_HALO, HALOS_PER_GROUP)).astype(jnp.int32)
    feedback = jnp.clip(0.5 + 1.0 * jax.random.uniform(streams_of[6], (N_HALO, HALOS_PER_GROUP), jnp.float32) ** level_of(streams_of[6], (N_HALO, HALOS_PER_GROUP), ((0, 4), (1, 64)), -0.2, 0.2), 0.5, 1.5)
    mixing = gaussian(streams_of[7], (3, K, K), K ** -0.5, 0.5, jnp.float32)
    drive = jnp.clip(jax.random.uniform(streams_of[8], (3, K), jnp.float32, 0.2, 1.0), 0.2, 1.0)
    readout = gaussian(streams_of[9], (3, K), 0.3, 1.5, jnp.float32)
    return dict(positions=positions, masses=masses, centres=centres, pair_halo=pair_halo, pair_tile=pair_tile, halo_slot=halo_slot, feedback=feedback, mixing=mixing, drive=drive, readout=readout)


def spline_basis(offset, knots):
    radial_distance = jnp.sqrt(lax.optimization_barrier(jnp.sum(offset * offset, axis=0)))
    scaled = radial_distance * ((knots - 1) / 2.6)
    knot_index = jnp.arange(knots, dtype=jnp.float32)
    return jnp.maximum(0.0, 1.0 - jnp.abs(scaled[..., None] - knot_index))

def relax(level, phi, mixing, drive, readout):
    state = jnp.zeros((3,) + level.shape, jnp.float32)
    for relax_iteration in range(ITERS):
        average = lax.optimization_barrier(jnp.mean(state, axis=0))
        fresh = []
        for comp in range(3):
            mixed = jnp.dot(state[comp], mixing[comp], precision=lax.Precision.HIGHEST)
            fresh.append(jnp.tanh(drive[comp] * level + phi[:, None] * mixed + 0.5 * average))
        state = jnp.stack(fresh)
    return lax.optimization_barrier(jnp.sum(state * readout[:, None, :], axis=0))

def reference(positions, masses, centres, pair_halo, pair_tile, halo_slot, feedback, mixing, drive, readout):
    tile_total = TILES_DEV * N_SPACE
    places = positions.reshape(3, tile_total, BLK)
    weights = masses.reshape(tile_total, BLK)
    block = math.gcd(PAIRS, 256)
    total = jnp.zeros((tile_total, 3, BLK), jnp.float32)
    for group in range(N_HALO):
        halo_ids = pair_halo[group]
        owner_space = jnp.arange(PAIRS, dtype=jnp.int32) // PAIRS_DEV
        tile_ids = (owner_space * TILES_DEV + pair_tile[group]).astype(jnp.int32)
        centre_rows = centres[group]

        def project(indices):
            halo_part, tile_part = indices
            offset = places[:, tile_part, :] - centre_rows[:, halo_part][:, :, None]
            basis = spline_basis(offset, K)
            return lax.optimization_barrier(jnp.sum(weights[tile_part][:, :, None] * basis, axis=1))
        pair_rows = lax.map(project, (halo_ids.reshape(-1, block), tile_ids.reshape(-1, block)))
        pair_rows = pair_rows.reshape(PAIRS, K)
        profile = jax.ops.segment_sum(pair_rows, halo_ids, num_segments=HALOS_PER_GROUP)
        level = jnp.log1p(profile)
        phi = feedback[group][halo_slot[group]]
        coef = relax(level, phi, mixing, drive, readout)

        def evaluate(indices):
            halo_part, tile_part = indices
            offset = places[:, tile_part, :] - centre_rows[:, halo_part][:, :, None]
            basis = spline_basis(offset, K)
            scalar = lax.optimization_barrier(jnp.sum(basis * coef[halo_part][:, None, :], axis=2))
            return jnp.transpose(offset * scalar[None], (1, 0, 2))
        shifted_positions = lax.map(evaluate, (halo_ids.reshape(-1, block), tile_ids.reshape(-1, block)))
        shifted_positions = shifted_positions.reshape(PAIRS, 3, BLK)
        total = total + jax.ops.segment_sum(shifted_positions, tile_ids, num_segments=tile_total)
    return jnp.transpose(total, (1, 0, 2)).reshape(3, PARTICLES)
```

```python
import functools

import jax
import jax.numpy as jnp
from jax import lax
from jax.experimental import pallas as pl
from jax.experimental.pallas import tpu as pltpu
from jax.sharding import PartitionSpec as P

BLK = 512
ITERS = 8
KNOTS = 128
TILES = 32
PAIRS = 256
HALOS = 1024
OWNED = 16
CHIPS = 32
GROUPS = 4
ROWS = CHIPS * OWNED
PER_GROUP = ROWS // GROUPS
LANES = 128
QUARTERS = BLK // LANES
SCALE = (KNOTS - 1) / 2.6
F32 = jnp.float32
BF16 = jnp.bfloat16
MESH = pl.DeviceIdType.MESH
VMEM = pl.BlockSpec(memory_space=pltpu.VMEM)


def two_parts(x):
    high = x.astype(BF16)
    return high, (x - high.astype(F32)).astype(BF16)


def three_parts(x):
    high = x.astype(BF16)
    rest = x - high.astype(F32)
    middle = rest.astype(BF16)
    return high, middle, (rest - middle.astype(F32)).astype(BF16)


def one_hot(mask):
    return jnp.where(mask, 1.0, 0.0).astype(BF16)


def matmul(a, b):
    return jnp.dot(a, b, preferred_element_type=F32)


def project_kernel(
    pos, mass, centre, halo, tile, slot, dense, offset, knot, fraction, columns,
    raw, parts, lookup, gathered, left, right, product, pair_rows,
):
    me = lax.axis_index("space")
    core, chip = lax.rem(me, 2), lax.div(me, 2)

    for t in range(TILES):
        for c in range(3):
            raw[t : t + 1, c * BLK : (c + 1) * BLK] = pos[c : c + 1, t * BLK : (t + 1) * BLK]
    for q in range(QUARTERS):
        raw[:, 3 * BLK + q * LANES : 3 * BLK + (q + 1) * LANES] = mass[pl.ds(q, TILES, stride=QUARTERS), :]
    for j, part in enumerate(three_parts(raw[...])):
        parts[j * TILES : (j + 1) * TILES, :] = part
    parts[3 * TILES :, :] = jnp.zeros((TILES, 4 * BLK), BF16)

    owner = slot[...] // OWNED
    half = lax.rem(lax.rem(owner, 2) - core + 2, 2)
    away = lax.rem(lax.div(owner, 2) - chip + CHIPS, CHIPS)
    row = half * ROWS + away * OWNED + lax.rem(slot[...], OWNED)
    lookup[...] = jnp.zeros_like(lookup)
    for j, part in enumerate(three_parts(centre[...])):
        lookup[3 * j : 3 * j + 3, :] = part.astype(F32)
    lookup[9:10, :] = lax.div(row, 32).astype(F32)
    lookup[10:11, :] = lax.rem(row, 32).astype(F32)
    halo_is = one_hot(lax.broadcasted_iota(jnp.int32, (HALOS, PAIRS), 0) == halo[...])
    found = matmul(lookup[...].astype(BF16), halo_is)
    pair_row = found[9:10] * 32.0 + found[10:11]
    by_pair = jnp.concatenate(
        [
            found[0:3] + found[3:6] + found[6:9],
            pair_row,
            tile[...].astype(F32),
            jnp.zeros((LANES - 5, PAIRS), F32),
        ],
        axis=0,
    )
    columns[...] = by_pair.T

    lane = lax.broadcasted_iota(jnp.int32, (PAIRS, LANES), 1)
    tile_is = one_hot(
        (lax.rem(lane, TILES).astype(F32) == columns[:, 4:5]) & (lane < 3 * TILES)
    )
    gathered[...] = matmul(tile_is, parts[...])

    lane8 = lax.broadcasted_iota(jnp.int32, (8, LANES), 1)
    sub8 = lax.broadcasted_iota(jnp.int32, (8, LANES), 0)
    low_lane = lax.rem(lane8, 16)

    def block(b, carry):
        rows = pl.ds(pl.multiple_of(b * 16, 16), 16)
        square = jnp.zeros((16, BLK), F32)
        for c in range(3):
            part = gathered[rows, c * BLK : (c + 1) * BLK] - columns[rows, c : c + 1]
            offset[c, rows, :] = part
            square += part * part
        scaled = jnp.sqrt(square) * SCALE
        below = jnp.floor(scaled)
        rest = scaled - below
        knot[rows, :] = below.astype(jnp.int32)
        fraction[rows, :] = rest
        coarse = jnp.floor(below * 0.125)
        fine = (below - 8.0 * coarse).astype(BF16)
        coarse = coarse.astype(BF16)
        weight = gathered[rows, 3 * BLK :]
        above = weight * rest
        w_below, w_above = two_parts(weight - above), two_parts(above)
        nothing, one = jnp.zeros((16, BLK), BF16), jnp.ones((16, BLK), BF16)
        masks = [fine == jnp.asarray(h, BF16) for h in range(8)]
        for j in range(2):
            for h in range(9):
                value = jnp.where(masks[h - 1], w_above[j], nothing) if h > 0 else nothing
                if h < 8:
                    value = jnp.where(masks[h], w_below[j], value)
                at = (j * 9 + h) * 16
                left[at : at + 16, :] = value
        for j in range(16):
            number = (j % 8) * 2 + j // 8
            right[j * 16 : j * 16 + 16, :] = jnp.where(coarse == jnp.asarray(number, BF16), one, nothing)
        product[...] = lax.dot_general(
            left[...], right[...], (((1,), (1,)), ((), ())), preferred_element_type=F32
        )
        for e in range(2):
            source = (lane8 - low_lane) + sub8 + 8 * e
            total = jnp.zeros((8, LANES), F32)
            for v in range(2):
                for h in range(9):
                    at = h * 16 + 8 * e
                    both = (
                        product[at : at + 8, v * LANES : (v + 1) * LANES]
                        + product[144 + at : 144 + at + 8, v * LANES : (v + 1) * LANES]
                    )
                    own = jnp.take_along_axis(both, source, axis=1)
                    to = 8 * v + h
                    if to == 16:
                        own = pltpu.roll(own, 16, 1)
                    total += jnp.where(low_lane == to % 16, own, 0.0)
            pair_rows[pl.ds(pl.multiple_of(b * 16 + 8 * e, 8), 8), :] = total
        return carry

    lax.fori_loop(0, PAIRS // 16, block, 0)

    row_is = one_hot(
        lax.broadcasted_iota(jnp.int32, (HALOS, PAIRS), 0) == pair_row.astype(jnp.int32)
    )
    both = matmul(row_is, jnp.concatenate(two_parts(pair_rows[...]), axis=1))
    dense[...] = both[:, :KNOTS] + both[:, KNOTS:]


def relax_kernel(
    dense, feedback, mixing, drive, readout, table,
    half_in, sums, sums_in, weights,
    half_send, half_recv, sums_send, sums_recv, coef_send, coef_recv, pass_send, pass_recv,
):
    me = lax.axis_index("space")
    core, chip = lax.rem(me, 2), lax.div(me, 2)
    sibling = {"space": chip * 2 + 1 - core}

    def at_chip(away):
        return {"space": lax.rem(chip + away + CHIPS, CHIPS) * 2 + core}

    barrier = pltpu.get_barrier_semaphore()
    pl.semaphore_signal(barrier, inc=1, device_id=sibling, device_id_type=MESH)
    for d in range(1, CHIPS):
        pl.semaphore_signal(barrier, inc=1, device_id=at_chip(d), device_id_type=MESH)
    for c in range(3):
        high, low = two_parts(mixing[c])
        weights[c, :KNOTS, :KNOTS] = high
        weights[c, KNOTS:, :KNOTS] = high
        weights[c, :KNOTS, KNOTS:] = low
        weights[c, KNOTS:, KNOTS:] = low
    eye = lax.broadcasted_iota(jnp.int32, (OWNED, OWNED), 0) == lax.broadcasted_iota(
        jnp.int32, (OWNED, OWNED), 1
    )
    phi = jnp.sum(jnp.where(eye, feedback[...], 0.0), axis=1, keepdims=True)
    pl.semaphore_wait(barrier, CHIPS)

    halves = []
    for q in range(GROUPS):
        copy = pltpu.make_async_remote_copy(
            src_ref=dense.at[pl.ds(ROWS + q * PER_GROUP, PER_GROUP)],
            dst_ref=half_in.at[pl.ds(q * PER_GROUP, PER_GROUP)],
            send_sem=half_send.at[q],
            recv_sem=half_recv.at[q],
            device_id=sibling,
            device_id_type=MESH,
        )
        copy.start()
        halves.append(copy)
    for q in range(GROUPS):
        halves[q].wait_recv()
        rows = pl.ds(q * PER_GROUP, PER_GROUP)
        sums[rows, :] = dense[rows, :] + half_in[rows, :]
        for d in range(max(1, q * 8), q * 8 + 8):
            pltpu.make_async_remote_copy(
                src_ref=sums.at[pl.ds(d * OWNED, OWNED)],
                dst_ref=sums_in.at[pl.ds((d - 1) * OWNED, OWNED)],
                send_sem=sums_send,
                recv_sem=sums_recv,
                device_id=at_chip(d),
                device_id_type=MESH,
            ).start()
    pltpu.make_async_copy(sums_in, sums_in, sums_recv).wait()
    owned = sums[0:OWNED, :]
    for d in range(1, CHIPS):
        owned += sums_in[(d - 1) * OWNED : d * OWNED, :]

    level = jnp.log1p(owned)
    driven = [drive[c : c + 1, :] * level for c in range(3)]
    state = [jnp.tanh(x) for x in driven]
    for _ in range(ITERS - 1):
        mean = (state[0] + state[1] + state[2]) * (0.5 / 3.0)
        fresh = []
        for c in range(3):
            mixed = matmul(jnp.concatenate(two_parts(state[c]), axis=1), weights[c])
            mixed = mixed[:, :KNOTS] + mixed[:, KNOTS:]
            fresh.append(jnp.tanh(driven[c] + phi * mixed + mean))
        state = fresh
    coef = readout[0:1, :] * state[0] + readout[1:2, :] * state[1] + readout[2:3, :] * state[2]

    table[0:OWNED, :] = coef
    for d in range(1, CHIPS):
        pltpu.make_async_remote_copy(
            src_ref=table.at[pl.ds(0, OWNED)],
            dst_ref=table.at[pl.ds(d * OWNED, OWNED)],
            send_sem=coef_send,
            recv_sem=coef_recv.at[d // 8],
            device_id=at_chip(-d),
            device_id_type=MESH,
        ).start()
    passed = []
    for q in range(GROUPS):
        first = OWNED if q == 0 else q * PER_GROUP
        arrived = table.at[pl.ds(first, (q + 1) * PER_GROUP - first)]
        pltpu.make_async_copy(arrived, arrived, coef_recv.at[q]).wait()
        copy = pltpu.make_async_remote_copy(
            src_ref=table.at[pl.ds(q * PER_GROUP, PER_GROUP)],
            dst_ref=table.at[pl.ds(ROWS + q * PER_GROUP, PER_GROUP)],
            send_sem=pass_send.at[q],
            recv_sem=pass_recv.at[q],
            device_id=sibling,
            device_id_type=MESH,
        )
        copy.start()
        passed.append(copy)
    for copy in passed:
        copy.wait_recv()
    for copy in halves + passed:
        copy.wait_send()
    sent = sums.at[pl.ds(OWNED, ROWS - OWNED)]
    pltpu.make_async_copy(sent, sent, sums_send).wait()
    pltpu.make_async_copy(sent, sent, coef_send).wait()


def evaluate_kernel(table, offset, knot, fraction, columns, tile, shares, coef_rows, moved):
    rows_of = lax.broadcasted_iota(jnp.int32, (PAIRS, HALOS), 1).astype(F32)
    row_is = one_hot(rows_of == columns[:, 3:4])
    both = matmul(row_is, jnp.concatenate(two_parts(table[...]), axis=1))
    coef_rows[...] = both[:, :KNOTS] + both[:, KNOTS:]

    def block(b, carry):
        rows = pl.ds(pl.multiple_of(b * 16, 16), 16)
        coef = coef_rows[rows, :]
        step = pltpu.roll(coef, KNOTS - 1, 1) - coef
        for q in range(QUARTERS):
            lanes = slice(q * LANES, (q + 1) * LANES)
            index = knot[rows, lanes]
            scalar = jnp.take_along_axis(coef, index, axis=1) + fraction[
                rows, lanes
            ] * jnp.take_along_axis(step, index, axis=1)
            for c in range(3):
                high, low = two_parts(offset[c, rows, lanes] * scalar)
                at = (q * 3 + c) * LANES
                moved[rows, at : at + LANES] = high
                moved[rows, 3 * BLK + at : 3 * BLK + at + LANES] = low
        return carry

    lax.fori_loop(0, PAIRS // 16, block, 0)
    tile_is = one_hot(lax.broadcasted_iota(jnp.int32, (TILES, PAIRS), 0) == tile[...])
    for q in range(QUARTERS):
        at = q * 3 * LANES
        share = matmul(tile_is, moved[:, at : at + 3 * LANES]) + matmul(
            tile_is, moved[:, 3 * BLK + at : 3 * BLK + at + 3 * LANES]
        )
        for c in range(3):
            shares[q, c * TILES : (c + 1) * TILES, :] = share[:, c * LANES : (c + 1) * LANES]


def combine_kernel(shares, out, share_in, total_in, total, share_send, share_recv, total_send, total_recv):
    me = lax.axis_index("halo")

    def peer(d):
        return {"halo": lax.rem(me + d + 4, 4)}

    barrier = pltpu.get_barrier_semaphore()
    for d in range(1, 4):
        pl.semaphore_signal(barrier, inc=1, device_id=peer(d), device_id_type=MESH)
    pl.semaphore_wait(barrier, 3)
    copies = []
    for d in (2, 1, 3):
        copy = pltpu.make_async_remote_copy(
            src_ref=shares.at[lax.rem(me + d, 4)],
            dst_ref=share_in.at[d - 1],
            send_sem=share_send.at[d - 1],
            recv_sem=share_recv.at[d - 1],
            device_id=peer(d),
            device_id_type=MESH,
        )
        copy.start()
        copies.append(copy)
    for copy in copies:
        copy.wait_recv()
    total[...] = shares[me] + share_in[0] + share_in[1] + share_in[2]
    for d in (2, 1, 3):
        copy = pltpu.make_async_remote_copy(
            src_ref=total,
            dst_ref=total_in.at[d - 1],
            send_sem=total_send.at[d - 1],
            recv_sem=total_recv.at[d - 1],
            device_id=peer(-d),
            device_id_type=MESH,
        )
        copy.start()
        copies.append(copy)

    def lay_out(block, quarter):
        for t in range(TILES):
            at = pl.ds(pl.multiple_of(t * BLK + quarter * LANES, LANES), LANES)
            for c in range(3):
                out[c : c + 1, at] = block[c * TILES + t : c * TILES + t + 1, :]

    lay_out(total, me)
    for d, copy in zip((2, 1, 3), copies[3:]):
        copy.wait_recv()
        lay_out(total_in.at[d - 1], lax.rem(me + d, 4))
    for copy in copies:
        copy.wait_send()


def call(kernel, outs, scratch, inputs, **params):
    return pl.pallas_call(
        kernel,
        out_shape=outs,
        in_specs=[VMEM] * inputs,
        out_specs=jax.tree.map(lambda _: VMEM, outs),
        scratch_shapes=scratch,
        compiler_params=pltpu.CompilerParams(vmem_limit_bytes=48 * 2**20, **params),
    )


def per_device(
    positions, masses, centres, pair_halo, pair_tile, halo_slot, feedback, mixing, drive, readout
):
    shape = jax.ShapeDtypeStruct
    dma = pltpu.SemaphoreType.DMA
    with jax.named_scope("project"):
        dense, offset, knot, fraction, columns = call(
            project_kernel,
            (
                shape((HALOS, KNOTS), F32),
                shape((3, PAIRS, BLK), F32),
                shape((PAIRS, BLK), jnp.int32),
                shape((PAIRS, BLK), F32),
                shape((PAIRS, LANES), F32),
            ),
            [
                pltpu.VMEM((TILES, 4 * BLK), F32),
                pltpu.VMEM((4 * TILES, 4 * BLK), BF16),
                pltpu.VMEM((16, HALOS), F32),
                pltpu.VMEM((PAIRS, 4 * BLK), F32),
                pltpu.VMEM((18 * 16, BLK), BF16),
                pltpu.VMEM((256, BLK), BF16),
                pltpu.VMEM((18 * 16, 256), F32),
                pltpu.VMEM((PAIRS, KNOTS), F32),
            ],
            6,
        )(
            positions,
            masses.reshape(QUARTERS * TILES, LANES),
            centres[0],
            pair_halo,
            pair_tile,
            halo_slot,
        )
    with jax.named_scope("relax"):
        table = call(
            relax_kernel,
            shape((HALOS, KNOTS), F32),
            [
                pltpu.VMEM((ROWS, KNOTS), F32),
                pltpu.VMEM((ROWS, KNOTS), F32),
                pltpu.VMEM((ROWS - OWNED, KNOTS), F32),
                pltpu.VMEM((3, 2 * KNOTS, 2 * KNOTS), BF16),
                dma((GROUPS,)),
                dma((GROUPS,)),
                dma,
                dma,
                dma,
                dma((GROUPS,)),
                dma((GROUPS,)),
                dma((GROUPS,)),
            ],
            5,
            collective_id=0,
            has_side_effects=True,
        )(dense, feedback, mixing, drive, readout)
    with jax.named_scope("evaluate"):
        shares = call(
            evaluate_kernel,
            shape((QUARTERS, 3 * TILES, LANES), F32),
            [pltpu.VMEM((PAIRS, KNOTS), F32), pltpu.VMEM((PAIRS, 6 * BLK), BF16)],
            6,
        )(table, offset, knot, fraction, columns, pair_tile)
    with jax.named_scope("combine"):
        return call(
            combine_kernel,
            shape((3, TILES * BLK), F32),
            [
                pltpu.VMEM((3, 3 * TILES, LANES), F32),
                pltpu.VMEM((3, 3 * TILES, LANES), F32),
                pltpu.VMEM((3 * TILES, LANES), F32),
                dma((3,)),
                dma((3,)),
                dma((3,)),
                dma((3,)),
            ],
            1,
            collective_id=1,
            has_side_effects=True,
        )(shares)


def solution(mesh):
    return jax.shard_map(
        per_device,
        mesh=mesh,
        in_specs=(
            P(None, "space"),
            P("space"),
            P("halo", None, None),
            P("halo", "space"),
            P("halo", "space"),
            P("halo", None),
            P("halo", "space"),
            P(),
            P(),
            P(),
        ),
        out_specs=P(None, "space"),
        check_vma=False,
    )
```

```python
import jax
import jax.numpy as jnp
from jax import lax
from jax.experimental import pallas as pl
from jax.experimental.pallas import tpu as pltpu
from jax.sharding import PartitionSpec as P

BLK = 512
ITERS = 8
KNOTS = 128
TILES = 32
PAIRS = 256
HALOS = 1024
OWNED = 16
N_Y = 4
N_Z = 8
N_X = 4
LINE = N_Z * OWNED
ROWS = N_Y * LINE
LANES = 128
QUARTERS = BLK // LANES
SCALE = (KNOTS - 1) / 2.6
F32 = jnp.float32
BF16 = jnp.bfloat16
MESH = pl.DeviceIdType.MESH


def two_parts(x):
    high = x.astype(BF16)
    return high, (x - high.astype(F32)).astype(BF16)


def three_parts(x):
    high = x.astype(BF16)
    rest = x - high.astype(F32)
    middle = rest.astype(BF16)
    return high, middle, (rest - middle.astype(F32)).astype(BF16)


def one_hot(mask):
    return jnp.where(mask, 1.0, 0.0).astype(BF16)


def matmul(a, b):
    return jnp.dot(a, b, preferred_element_type=F32)


def kernel(
    pos_in, mass_in, centre_in, halo_in, tile_in, slot_in, feedback_in, mixing_in, drive_in, readout_in,
    out,
    pos, mass, centre, halo, tile, slot, feedback, mixing, drive, readout, loaded,
    raw, parts, lookup, gathered, columns, offset, knot, fraction, left, right, product, pair_rows,
    dense, half_in, sums, y_in, z_sums, z_in, weights, table, coef_rows, moved, shares, share_in, total, total_in,
    half_send, half_recv, y_send, y_recv, z_send, z_recv,
    coef_z_send, coef_z_recv, coef_y_send, coef_y_recv, pass_send, pass_recv,
    share_send, share_recv, total_send, total_recv,
):
    inputs = (pos_in, mass_in, centre_in, halo_in, tile_in, slot_in, feedback_in, mixing_in, drive_in, readout_in)
    copies_in = [
        pltpu.make_async_copy(source, target, loaded.at[i])
        for i, (source, target) in enumerate(
            zip(inputs, (pos, mass, centre, halo, tile, slot, feedback, mixing, drive, readout))
        )
    ]
    for copy in copies_in:
        copy.start()

    me = lax.axis_index("space")
    x = lax.axis_index("halo")
    core, y, z = lax.rem(me, 2), lax.rem(lax.div(me, 2), N_Y), lax.div(me, 2 * N_Y)

    def at(dz=0, dy=0, other=0):
        place = lax.rem(z + dz + N_Z, N_Z) * N_Y + lax.rem(y + dy + N_Y, N_Y)
        return {"space": place * 2 + (1 - core if other else core)}

    def beside(d):
        return {"halo": lax.rem(x + d + N_X, N_X)}

    def send(source, target, send_sem, recv_sem, device):
        copy = pltpu.make_async_remote_copy(
            src_ref=source,
            dst_ref=target,
            send_sem=send_sem,
            recv_sem=recv_sem,
            device_id=device,
            device_id_type=MESH,
        )
        copy.start()
        return copy

    def wait_bytes(ref, sem):
        pltpu.make_async_copy(ref, ref, sem).wait()

    barrier = pltpu.get_barrier_semaphore()
    partners = [at(other=1)]
    partners += [at(dy=d) for d in range(1, N_Y)]
    partners += [at(dz=d) for d in range(1, N_Z)]
    partners += [beside(d) for d in range(1, N_X)]
    for partner in partners:
        pl.semaphore_signal(barrier, inc=1, device_id=partner, device_id_type=MESH)

    for i in (2, 3, 4, 5):
        copies_in[i].wait()
    owner = lax.div(slot[...], OWNED)
    half = lax.rem(lax.rem(owner, 2) - core + 2, 2)
    far_y = lax.rem(lax.rem(lax.div(owner, 2), N_Y) - y + N_Y, N_Y)
    far_z = lax.rem(lax.div(owner, 2 * N_Y) - z + N_Z, N_Z)
    row = half * ROWS + far_y * LINE + far_z * OWNED + lax.rem(slot[...], OWNED)
    lookup[...] = jnp.zeros_like(lookup)
    for j, part in enumerate(three_parts(centre[0])):
        lookup[3 * j : 3 * j + 3, :] = part.astype(F32)
    lookup[9:10, :] = lax.div(row, 32).astype(F32)
    lookup[10:11, :] = lax.rem(row, 32).astype(F32)
    halo_is = one_hot(lax.broadcasted_iota(jnp.int32, (HALOS, PAIRS), 0) == halo[...])
    found = matmul(lookup[...].astype(BF16), halo_is)
    pair_row = found[9:10] * 32.0 + found[10:11]
    by_pair = jnp.concatenate(
        [
            found[0:3] + found[3:6] + found[6:9],
            pair_row,
            tile[...].astype(F32),
            jnp.zeros((LANES - 5, PAIRS), F32),
        ],
        axis=0,
    )
    columns[...] = by_pair.T

    for i in (0, 1):
        copies_in[i].wait()
    for t in range(TILES):
        for c in range(3):
            raw[t : t + 1, c * BLK : (c + 1) * BLK] = pos[c : c + 1, t * BLK : (t + 1) * BLK]
    for q in range(QUARTERS):
        raw[:, 3 * BLK + q * LANES : 3 * BLK + (q + 1) * LANES] = mass[pl.ds(q, TILES, stride=QUARTERS), :]
    for j, part in enumerate(three_parts(raw[...])):
        parts[j * TILES : (j + 1) * TILES, :] = part
    parts[3 * TILES :, :] = jnp.zeros((TILES, 4 * BLK), BF16)
    lane = lax.broadcasted_iota(jnp.int32, (PAIRS, LANES), 1)
    tile_is = one_hot((lax.rem(lane, TILES).astype(F32) == columns[:, 4:5]) & (lane < 3 * TILES))
    gathered[...] = matmul(tile_is, parts[...])

    lane8 = lax.broadcasted_iota(jnp.int32, (8, LANES), 1)
    sub8 = lax.broadcasted_iota(jnp.int32, (8, LANES), 0)
    low_lane = lax.rem(lane8, 16)

    def build(start, u):
        rows = pl.ds(pl.multiple_of(start, 16), 16)
        square = jnp.zeros((16, BLK), F32)
        for c in range(3):
            part = gathered[rows, c * BLK : (c + 1) * BLK] - columns[rows, c : c + 1]
            offset[c, rows, :] = part
            square += part * part
        scaled = jnp.sqrt(square) * SCALE
        below = jnp.floor(scaled)
        rest = scaled - below
        knot[rows, :] = below.astype(jnp.int32)
        fraction[rows, :] = rest
        coarse = jnp.floor(below * 0.125)
        fine = (below - 8.0 * coarse).astype(BF16)
        coarse = coarse.astype(BF16)
        weight = gathered[rows, 3 * BLK :]
        above = weight * rest
        w_below, w_above = two_parts(weight - above), two_parts(above)
        nothing, one = jnp.zeros((16, BLK), BF16), jnp.ones((16, BLK), BF16)
        masks = [fine == jnp.asarray(h, BF16) for h in range(8)]
        for j in range(2):
            for h in range(9):
                value = jnp.where(masks[h - 1], w_above[j], nothing) if h > 0 else nothing
                if h < 8:
                    value = jnp.where(masks[h], w_below[j], value)
                spot = (j * 9 + h) * 16
                left[u, spot : spot + 16, :] = value
        for j in range(16):
            number = (j % 8) * 2 + j // 8
            right[u, j * 16 : j * 16 + 16, :] = jnp.where(coarse == jnp.asarray(number, BF16), one, nothing)

    def fold(start, u):
        for e in range(2):
            source = (lane8 - low_lane) + sub8 + 8 * e
            profile = jnp.zeros((8, LANES), F32)
            for v in range(2):
                for h in range(9):
                    spot = h * 16 + 8 * e
                    both = (
                        product[u, spot : spot + 8, v * LANES : (v + 1) * LANES]
                        + product[u, 144 + spot : 144 + spot + 8, v * LANES : (v + 1) * LANES]
                    )
                    own = jnp.take_along_axis(both, source, axis=1)
                    to = 8 * v + h
                    if to == 16:
                        own = pltpu.roll(own, 16, 1)
                    profile += jnp.where(low_lane == to % 16, own, 0.0)
            pair_rows[pl.ds(pl.multiple_of(start + 8 * e, 8), 8), :] = profile

    def block(b, carry):
        for u in range(2):
            build(b * 32 + u * 16, u)
        for u in range(2):
            product[u] = lax.dot_general(
                left[u], right[u], (((1,), (1,)), ((), ())), preferred_element_type=F32
            )
        for u in range(2):
            fold(b * 32 + u * 16, u)
        return carry

    lax.fori_loop(0, PAIRS // 32, block, 0)

    row_is = one_hot(lax.broadcasted_iota(jnp.int32, (HALOS, PAIRS), 0) == pair_row.astype(jnp.int32))
    both = matmul(row_is, jnp.concatenate(two_parts(pair_rows[...]), axis=1))
    dense[...] = both[:, :KNOTS] + both[:, KNOTS:]

    pl.semaphore_wait(barrier, len(partners))
    halves = {}
    for d in (2, 1, 3, 0):
        halves[d] = send(
            dense.at[pl.ds(ROWS + d * LINE, LINE)],
            half_in.at[pl.ds(d * LINE, LINE)],
            half_send.at[d],
            half_recv.at[d],
            at(other=1),
        )
    for i in (6, 7, 8, 9):
        copies_in[i].wait()
    for c in range(3):
        high, low = two_parts(mixing[c])
        weights[c, :KNOTS, :KNOTS] = high
        weights[c, KNOTS:, :KNOTS] = high
        weights[c, :KNOTS, KNOTS:] = low
        weights[c, KNOTS:, KNOTS:] = low
    eye = lax.broadcasted_iota(jnp.int32, (OWNED, OWNED), 0) == lax.broadcasted_iota(
        jnp.int32, (OWNED, OWNED), 1
    )
    phi = jnp.sum(jnp.where(eye, feedback[...], 0.0), axis=1, keepdims=True)

    along_y = []
    for d in (2, 1, 3, 0):
        halves[d].wait_recv()
        rows = pl.ds(d * LINE, LINE)
        sums[rows, :] = dense[rows, :] + half_in[rows, :]
        if d > 0:
            for part in (1, 0):
                along_y.append(
                    send(
                        sums.at[pl.ds(d * LINE + part * LINE // 2, LINE // 2)],
                        y_in.at[pl.ds((d - 1) * LINE + part * LINE // 2, LINE // 2)],
                        y_send.at[part, d - 1],
                        y_recv.at[part, d - 1],
                        at(dy=d),
                    )
                )
    for part in (1, 0):
        for i, d in enumerate((2, 1, 3)):
            along_y[2 * i + (1 - part)].wait_recv()
        first = part * LINE // 2
        rows = pl.ds(first, LINE // 2)
        line = sums[rows, :]
        for d in range(1, N_Y):
            line += y_in[pl.ds((d - 1) * LINE + first, LINE // 2), :]
        z_sums[rows, :] = line
        for d in range(4 * part, 4 * part + 4):
            if d > 0:
                send(
                    z_sums.at[pl.ds(d * OWNED, OWNED)],
                    z_in.at[pl.ds((d - 1) * OWNED, OWNED)],
                    z_send,
                    z_recv,
                    at(dz=d),
                )
    wait_bytes(z_in, z_recv)
    owned = z_sums[0:OWNED, :]
    for d in range(1, N_Z):
        owned += z_in[(d - 1) * OWNED : d * OWNED, :]

    level = jnp.log1p(owned)
    driven = [drive[c : c + 1, :] * level for c in range(3)]
    state = [jnp.tanh(v) for v in driven]
    for _ in range(ITERS - 1):
        mean = (state[0] + state[1] + state[2]) * (0.5 / 3.0)
        fresh = []
        for c in range(3):
            mixed = matmul(jnp.concatenate(two_parts(state[c]), axis=1), weights[c])
            mixed = mixed[:, :KNOTS] + mixed[:, KNOTS:]
            fresh.append(jnp.tanh(driven[c] + phi * mixed + mean))
        state = fresh
    table[0:OWNED, :] = (
        readout[0:1, :] * state[0] + readout[1:2, :] * state[1] + readout[2:3, :] * state[2]
    )

    for d in range(1, N_Z):
        send(
            table.at[pl.ds(0, OWNED)],
            table.at[pl.ds(d * OWNED, OWNED)],
            coef_z_send,
            coef_z_recv.at[d // 4],
            at(dz=-d),
        )
    lines = []
    for part in range(2):
        first = OWNED if part == 0 else LINE // 2
        wait_bytes(table.at[pl.ds(first, (part + 1) * LINE // 2 - first)], coef_z_recv.at[part])
        for d in (2, 1, 3):
            lines.append(
                send(
                    table.at[pl.ds(part * LINE // 2, LINE // 2)],
                    table.at[pl.ds(d * LINE + part * LINE // 2, LINE // 2)],
                    coef_y_send.at[part, d - 1],
                    coef_y_recv.at[part, d - 1],
                    at(dy=-d),
                )
            )
    passed = []
    for d in (0, 1, 3, 2):
        if d > 0:
            for part in range(2):
                lines[3 * part + (2, 1, 3).index(d)].wait_recv()
        passed.append(
            send(
                table.at[pl.ds(d * LINE, LINE)],
                table.at[pl.ds(ROWS + d * LINE, LINE)],
                pass_send.at[d],
                pass_recv.at[d],
                at(other=1),
            )
        )
    for copy in passed:
        copy.wait_recv()

    rows_of = lax.broadcasted_iota(jnp.int32, (PAIRS, HALOS), 1).astype(F32)
    both = matmul(one_hot(rows_of == columns[:, 3:4]), jnp.concatenate(two_parts(table[...]), axis=1))
    coef_rows[...] = both[:, :KNOTS] + both[:, KNOTS:]
    tile_is = one_hot(lax.broadcasted_iota(jnp.int32, (TILES, PAIRS), 0) == tile[...])

    combined = []
    for d in (2, 1, 3, 0):
        lanes = pl.ds(pl.multiple_of(lax.rem(x + d, N_X) * LANES, LANES), LANES)

        def evaluate(b, carry):
            rows = pl.ds(pl.multiple_of(b * 16, 16), 16)
            coef = coef_rows[rows, :]
            step = pltpu.roll(coef, KNOTS - 1, 1) - coef
            index = knot[rows, lanes]
            scalar = jnp.take_along_axis(coef, index, axis=1) + fraction[
                rows, lanes
            ] * jnp.take_along_axis(step, index, axis=1)
            for c in range(3):
                high, low = two_parts(offset[c, rows, lanes] * scalar)
                moved[rows, c * LANES : (c + 1) * LANES] = high
                moved[rows, (c + 3) * LANES : (c + 4) * LANES] = low
            return carry

        lax.fori_loop(0, PAIRS // 16, evaluate, 0, unroll=4)
        share = matmul(tile_is, moved[...])
        for c in range(3):
            shares[d, c * TILES : (c + 1) * TILES, :] = (
                share[:, c * LANES : (c + 1) * LANES] + share[:, (c + 3) * LANES : (c + 4) * LANES]
            )
        if d > 0:
            combined.append(
                send(shares.at[d], share_in.at[d - 1], share_send.at[d - 1], share_recv.at[d - 1], beside(d))
            )
    for copy in combined:
        copy.wait_recv()
    total[...] = shares[0] + share_in[0] + share_in[1] + share_in[2]
    finished = [
        send(total, total_in.at[d - 1], total_send.at[d - 1], total_recv.at[d - 1], beside(-d)) for d in (2, 1, 3)
    ]

    def lay_out(part, quarter):
        for t in range(TILES):
            lanes = pl.ds(pl.multiple_of(t * BLK + quarter * LANES, LANES), LANES)
            for c in range(3):
                out[c : c + 1, lanes] = part[c * TILES + t : c * TILES + t + 1, :]

    lay_out(total, x)
    for d, copy in zip((2, 1, 3), finished):
        copy.wait_recv()
        lay_out(total_in.at[d - 1], lax.rem(x + d, N_X))
    for copy in (*halves.values(), *along_y, *lines, *passed, *combined, *finished):
        copy.wait_send()
    wait_bytes(z_in, z_send)
    wait_bytes(z_in, coef_z_send)


def per_device(
    positions, masses, centres, pair_halo, pair_tile, halo_slot, feedback, mixing, drive, readout
):
    dma = pltpu.SemaphoreType.DMA
    vmem = pltpu.VMEM
    args = (
        positions,
        masses.reshape(QUARTERS * TILES, LANES),
        centres,
        pair_halo,
        pair_tile,
        halo_slot,
        feedback,
        mixing,
        drive,
        readout,
    )
    share = (3 * TILES, LANES)
    return pl.pallas_call(
        kernel,
        out_shape=jax.ShapeDtypeStruct(positions.shape, F32),
        in_specs=[pl.BlockSpec(memory_space=pl.ANY)] * len(args),
        out_specs=pl.BlockSpec(memory_space=vmem),
        scratch_shapes=[
            *(vmem(a.shape, a.dtype) for a in args),
            dma((len(args),)),
            vmem((TILES, 4 * BLK), F32),
            vmem((4 * TILES, 4 * BLK), BF16),
            vmem((16, HALOS), F32),
            vmem((PAIRS, 4 * BLK), F32),
            vmem((PAIRS, LANES), F32),
            vmem((3, PAIRS, BLK), F32),
            vmem((PAIRS, BLK), jnp.int32),
            vmem((PAIRS, BLK), F32),
            vmem((2, 18 * 16, BLK), BF16),
            vmem((2, 256, BLK), BF16),
            vmem((2, 18 * 16, 256), F32),
            vmem((PAIRS, KNOTS), F32),
            vmem((HALOS, KNOTS), F32),
            vmem((ROWS, KNOTS), F32),
            vmem((ROWS, KNOTS), F32),
            vmem((ROWS - LINE, KNOTS), F32),
            vmem((LINE, KNOTS), F32),
            vmem((LINE - OWNED, KNOTS), F32),
            vmem((3, 2 * KNOTS, 2 * KNOTS), BF16),
            vmem((HALOS, KNOTS), F32),
            vmem((PAIRS, KNOTS), F32),
            vmem((PAIRS, 6 * LANES), BF16),
            vmem((N_X, *share), F32),
            vmem((N_X - 1, *share), F32),
            vmem(share, F32),
            vmem((N_X - 1, *share), F32),
            dma((N_Y,)),
            dma((N_Y,)),
            dma((2, N_Y - 1)),
            dma((2, N_Y - 1)),
            dma,
            dma,
            dma,
            dma((2,)),
            dma((2, N_Y - 1)),
            dma((2, N_Y - 1)),
            dma((N_Y,)),
            dma((N_Y,)),
            dma((N_X - 1,)),
            dma((N_X - 1,)),
            dma((N_X - 1,)),
            dma((N_X - 1,)),
        ],
        compiler_params=pltpu.CompilerParams(
            vmem_limit_bytes=48 * 2**20, collective_id=0, has_side_effects=True
        ),
    )(*args)


def solution(mesh):
    return jax.shard_map(
        per_device,
        mesh=mesh,
        in_specs=(
            P(None, "space"),
            P("space"),
            P("halo", None, None),
            P("halo", "space"),
            P("halo", "space"),
            P("halo", None),
            P("halo", "space"),
            P(),
            P(),
            P(),
        ),
        out_specs=P(None, "space"),
        check_vma=False,
    )
```

```python
import jax
import jax.numpy as jnp
from jax import lax
from jax.experimental import pallas as pl
from jax.experimental.pallas import tpu as pltpu
from jax.sharding import PartitionSpec as P

BLK = 512
ITERS = 8
KNOTS = 128
TILES = 32
PAIRS = 256
HALOS = 1024
OWNED = 16
N_Y = 4
N_Z = 8
N_X = 4
PLANE = N_Y * OWNED
ROWS = N_Z * PLANE
STEPS = N_Z // 2
ORDER = (4, 3, 5, 2, 6, 1, 7, 0)
TURNS = ((7, 1), (6, 1), (4, 2), (2, 2), (0, 2))
TURNS_OF = (4, 4, 3, 3, 2, 2, 1)
LANES = 128
QUARTERS = BLK // LANES
VMEM_BYTES = 60 * 2**20
SCALE = (KNOTS - 1) / 2.6
F32 = jnp.float32
BF16 = jnp.bfloat16
MESH = pl.DeviceIdType.MESH


def two_parts(x):
    high = x.astype(BF16)
    return high, (x - high.astype(F32)).astype(BF16)


def three_parts(x):
    high = x.astype(BF16)
    rest = x - high.astype(F32)
    middle = rest.astype(BF16)
    return high, middle, (rest - middle.astype(F32)).astype(BF16)


def one_hot(mask):
    return jnp.where(mask, 1.0, 0.0).astype(BF16)


def matmul(a, b):
    return jnp.dot(a, b, preferred_element_type=F32)


def kernel(
    pos_in, mass_in, centre_in, halo_in, tile_in, slot_in, feedback_in, mixing_in, drive_in, readout_in,
    out,
    pos, mass, centre, halo, tile, slot, feedback, mixing, drive, readout, loaded,
    raw, parts, lookup, gathered, columns, offset, knot, fraction, left, right, product, pair_rows,
    dense, half_in, sums, y_in, z_sums, z_in, weights, table, coef_rows, moved, shares, share_in, total, total_in,
    half_send, half_recv, y_send, y_recv, z_send, z_recv,
    coef_z_send, coef_z_recv, coef_y_send, coef_y_recv, pass_send, pass_recv,
    share_send, share_recv, total_send, total_recv,
):
    inputs = (pos_in, mass_in, centre_in, halo_in, tile_in, slot_in, feedback_in, mixing_in, drive_in, readout_in)
    copies_in = [
        pltpu.make_async_copy(source, target, loaded.at[i])
        for i, (source, target) in enumerate(
            zip(inputs, (pos, mass, centre, halo, tile, slot, feedback, mixing, drive, readout))
        )
    ]
    for copy in copies_in:
        copy.start()

    me = lax.axis_index("space")
    x = lax.axis_index("halo")
    core, y, z = lax.rem(me, 2), lax.rem(lax.div(me, 2), N_Y), lax.div(me, 2 * N_Y)

    def at(dz=0, dy=0, other=0):
        place = lax.rem(z + dz + N_Z, N_Z) * N_Y + lax.rem(y + dy + N_Y, N_Y)
        return {"space": place * 2 + (1 - core if other else core)}

    def beside(d):
        return {"halo": lax.rem(x + d + N_X, N_X)}

    def send(source, target, send_sem, recv_sem, device):
        copy = pltpu.make_async_remote_copy(
            src_ref=source,
            dst_ref=target,
            send_sem=send_sem,
            recv_sem=recv_sem,
            device_id=device,
            device_id_type=MESH,
        )
        copy.start()
        return copy

    def wait_bytes(ref, sem):
        pltpu.make_async_copy(ref, ref, sem).wait()

    barrier = pltpu.get_barrier_semaphore()
    partners = [at(other=1)]
    partners += [at(dy=d) for d in range(1, N_Y)]
    partners += [at(dz=d) for d in range(1, N_Z)]
    partners += [beside(d) for d in range(1, N_X)]
    for partner in partners:
        pl.semaphore_signal(barrier, inc=1, device_id=partner, device_id_type=MESH)

    for i in (2, 3, 4, 5):
        copies_in[i].wait()
    owner = lax.div(slot[...], OWNED)
    half = lax.rem(lax.rem(owner, 2) - core + 2, 2)
    far_y = lax.rem(lax.rem(lax.div(owner, 2), N_Y) - y + N_Y, N_Y)
    far_z = lax.rem(lax.div(owner, 2 * N_Y) - z + N_Z, N_Z)
    turn = jnp.where(far_z < N_Z // 2, N_Z - 1 - 2 * far_z, 2 * far_z - N_Z)
    row = half * ROWS + turn * PLANE + far_y * OWNED + lax.rem(slot[...], OWNED)
    lookup[...] = jnp.zeros_like(lookup)
    for j, part in enumerate(three_parts(centre[...])):
        part = part.astype(F32)
        for c in range(3):
            for i in range(HALOS // LANES):
                at_row = c * (HALOS // LANES) + i
                lookup[3 * j + c : 3 * j + c + 1, i * LANES : (i + 1) * LANES] = part[at_row : at_row + 1, :]
    lookup[9:10, :] = lax.div(row, 32).astype(F32)
    lookup[10:11, :] = lax.rem(row, 32).astype(F32)
    halo_is = one_hot(lax.broadcasted_iota(jnp.int32, (HALOS, PAIRS), 0) == halo[...])
    found = matmul(lookup[...].astype(BF16), halo_is)
    pair_row = found[9:10] * 32.0 + found[10:11]
    by_pair = jnp.concatenate(
        [
            found[0:3] + found[3:6] + found[6:9],
            pair_row,
            tile[...].astype(F32),
            jnp.zeros((LANES - 5, PAIRS), F32),
        ],
        axis=0,
    )
    columns[...] = by_pair.T

    for i in (0, 1):
        copies_in[i].wait()
    for t in range(TILES):
        for c in range(3):
            raw[t : t + 1, c * BLK : (c + 1) * BLK] = pos[c : c + 1, t * BLK : (t + 1) * BLK]
    for q in range(QUARTERS):
        raw[:, 3 * BLK + q * LANES : 3 * BLK + (q + 1) * LANES] = mass[pl.ds(q, TILES, stride=QUARTERS), :]
    for j, part in enumerate(three_parts(raw[...])):
        parts[j * TILES : (j + 1) * TILES, :] = part
    parts[3 * TILES :, :] = jnp.zeros((TILES, 4 * BLK), BF16)
    lane = lax.broadcasted_iota(jnp.int32, (PAIRS, LANES), 1)
    tile_is = one_hot((lax.rem(lane, TILES).astype(F32) == columns[:, 4:5]) & (lane < 3 * TILES))
    gathered[...] = matmul(tile_is, parts[...])

    lane8 = lax.broadcasted_iota(jnp.int32, (8, LANES), 1)
    sub8 = lax.broadcasted_iota(jnp.int32, (8, LANES), 0)
    low_lane = lax.rem(lane8, 16)

    def build(start, u):
        rows = pl.ds(pl.multiple_of(start, 16), 16)
        square = jnp.zeros((16, BLK), F32)
        for c in range(3):
            part = gathered[rows, c * BLK : (c + 1) * BLK] - columns[rows, c : c + 1]
            offset[c, rows, :] = part
            square += part * part
        scaled = jnp.sqrt(square) * SCALE
        below = jnp.floor(scaled)
        rest = scaled - below
        knot[rows, :] = below.astype(jnp.int32)
        fraction[rows, :] = rest
        coarse = jnp.floor(below * 0.125)
        fine = (below - 8.0 * coarse).astype(BF16)
        coarse = coarse.astype(BF16)
        weight = gathered[rows, 3 * BLK :]
        above = weight * rest
        w_below, w_above = two_parts(weight - above), two_parts(above)
        nothing, one = jnp.zeros((16, BLK), BF16), jnp.ones((16, BLK), BF16)
        masks = [fine == jnp.asarray(h, BF16) for h in range(8)]
        for j in range(2):
            for h in range(9):
                value = jnp.where(masks[h - 1], w_above[j], nothing) if h > 0 else nothing
                if h < 8:
                    value = jnp.where(masks[h], w_below[j], value)
                spot = (j * 9 + h) * 16
                left[u, spot : spot + 16, :] = value
        for j in range(16):
            number = (j % 8) * 2 + j // 8
            right[u, j * 16 : j * 16 + 16, :] = jnp.where(coarse == jnp.asarray(number, BF16), one, nothing)

    def fold(start, u):
        for e in range(2):
            source = (lane8 - low_lane) + sub8 + 8 * e
            profile = jnp.zeros((8, LANES), F32)
            for v in range(2):
                for h in range(9):
                    spot = h * 16 + 8 * e
                    both = (
                        product[u, spot : spot + 8, v * LANES : (v + 1) * LANES]
                        + product[u, 144 + spot : 144 + spot + 8, v * LANES : (v + 1) * LANES]
                    )
                    own = jnp.take_along_axis(both, source, axis=1)
                    to = 8 * v + h
                    if to == 16:
                        own = pltpu.roll(own, 16, 1)
                    profile += jnp.where(low_lane == to % 16, own, 0.0)
            pair_rows[pl.ds(pl.multiple_of(start + 8 * e, 8), 8), :] = profile

    def block(b, carry):
        for u in range(2):
            build(b * 32 + u * 16, u)
        for u in range(2):
            product[u] = lax.dot_general(
                left[u], right[u], (((1,), (1,)), ((), ())), preferred_element_type=F32
            )
        for u in range(2):
            fold(b * 32 + u * 16, u)
        return carry

    lax.fori_loop(0, PAIRS // 32, block, 0)

    row_is = one_hot(lax.broadcasted_iota(jnp.int32, (HALOS, PAIRS), 0) == pair_row.astype(jnp.int32))
    both = matmul(row_is, jnp.concatenate(two_parts(pair_rows[...]), axis=1))
    dense[...] = (both[:, :KNOTS] + both[:, KNOTS:]).reshape(2 * N_Z, PLANE, KNOTS)

    pl.semaphore_wait(barrier, len(partners))
    halves = [
        send(
            dense.at[pl.ds(N_Z + 2 * j, 2)],
            half_in.at[pl.ds(2 * j, 2)],
            half_send.at[j],
            half_recv.at[j],
            at(other=1),
        )
        for j in range(STEPS)
    ]
    for i in (6, 7, 8, 9):
        copies_in[i].wait()
    for c in range(3):
        high, low = two_parts(mixing[c])
        weights[c, :KNOTS, :KNOTS] = high
        weights[c, KNOTS:, :KNOTS] = high
        weights[c, :KNOTS, KNOTS:] = low
        weights[c, KNOTS:, KNOTS:] = low
    eye = lax.broadcasted_iota(jnp.int32, (OWNED, OWNED), 0) == lax.broadcasted_iota(
        jnp.int32, (OWNED, OWNED), 1
    )
    phi = jnp.sum(jnp.where(eye, feedback[...], 0.0), axis=1, keepdims=True)

    for j in range(STEPS):
        halves[j].wait_recv()
        turns = pl.ds(2 * j, 2)
        sums[turns] = dense[turns] + half_in[turns]
        for d in (2, 1, 3):
            send(
                sums.at[turns, pl.ds(d * OWNED, OWNED)],
                y_in.at[j, d - 1],
                y_send,
                y_recv.at[j],
                at(dy=d),
            )
    for j in range(STEPS):
        wait_bytes(y_in.at[j], y_recv.at[j])
        plane = sums[2 * j : 2 * j + 2, :OWNED] + y_in[j, 0] + y_in[j, 1] + y_in[j, 2]
        z_sums[2 * j : 2 * j + 2] = plane
        for i in (2 * j, 2 * j + 1):
            if ORDER[i]:
                send(z_sums.at[i], z_in.at[i], z_send, z_recv, at(dz=ORDER[i]))
    wait_bytes(z_in, z_recv)
    owned = z_sums[N_Z - 1]
    for i in range(N_Z - 1):
        owned += z_in[i]

    level = jnp.log1p(owned)
    driven = [drive[c : c + 1, :] * level for c in range(3)]
    state = [jnp.tanh(v) for v in driven]
    for _ in range(ITERS - 1):
        mean = (state[0] + state[1] + state[2]) * (0.5 / 3.0)
        fresh = []
        for c in range(3):
            mixed = matmul(jnp.concatenate(two_parts(state[c]), axis=1), weights[c])
            mixed = mixed[:, :KNOTS] + mixed[:, KNOTS:]
            fresh.append(jnp.tanh(driven[c] + phi * mixed + mean))
        state = fresh
    table[N_Z - 1, :OWNED] = (
        readout[0:1, :] * state[0] + readout[1:2, :] * state[1] + readout[2:3, :] * state[2]
    )

    own = table.at[N_Z - 1, pl.ds(0, OWNED)]
    for i in reversed(range(N_Z - 1)):
        send(own, table.at[i, pl.ds(0, OWNED)], coef_z_send, coef_z_recv.at[TURNS_OF[i]], at(dz=-ORDER[i]))
    for g, (first, count) in enumerate(TURNS):
        line = table.at[pl.ds(first, count), pl.ds(0, OWNED)]
        if g > 0:
            wait_bytes(line, coef_z_recv.at[g])
        for d in (2, 1, 3):
            send(
                line,
                table.at[pl.ds(first, count), pl.ds(d * OWNED, OWNED)],
                coef_y_send,
                coef_y_recv.at[g],
                at(dy=-d),
            )
    passed = []
    for g, (first, count) in enumerate(TURNS):
        wait_bytes(table.at[pl.ds(first, count), pl.ds(OWNED, 3 * OWNED)], coef_y_recv.at[g])
        passed.append(
            send(
                table.at[pl.ds(first, count)],
                table.at[pl.ds(N_Z + first, count)],
                pass_send.at[g],
                pass_recv.at[g],
                at(other=1),
            )
        )

    def coefficients(first):
        rows_of = lax.broadcasted_iota(jnp.int32, (PAIRS, ROWS), 1).astype(F32) + first * float(ROWS)
        rows = table[first * N_Z : (first + 1) * N_Z].reshape(ROWS, KNOTS)
        both = matmul(one_hot(rows_of == columns[:, 3:4]), jnp.concatenate(two_parts(rows), axis=1))
        return both[:, :KNOTS] + both[:, KNOTS:]

    coef_rows[...] = coefficients(0)
    tile_is = one_hot(lax.broadcasted_iota(jnp.int32, (TILES, PAIRS), 0) == tile[...])
    for copy in passed:
        copy.wait_recv()
    coef_rows[...] += coefficients(1)

    combined = []
    for d in (2, 1, 3, 0):
        lanes = pl.ds(pl.multiple_of(lax.rem(x + d, N_X) * LANES, LANES), LANES)

        def evaluate(b, carry):
            rows = pl.ds(pl.multiple_of(b * 16, 16), 16)
            coef = coef_rows[rows, :]
            step = pltpu.roll(coef, KNOTS - 1, 1) - coef
            index = knot[rows, lanes]
            scalar = jnp.take_along_axis(coef, index, axis=1) + fraction[
                rows, lanes
            ] * jnp.take_along_axis(step, index, axis=1)
            for c in range(3):
                high, low = two_parts(offset[c, rows, lanes] * scalar)
                moved[rows, c * LANES : (c + 1) * LANES] = high
                moved[rows, (c + 3) * LANES : (c + 4) * LANES] = low
            return carry

        lax.fori_loop(0, PAIRS // 16, evaluate, 0, unroll=4)
        share = matmul(tile_is, moved[...])
        for c in range(3):
            shares[d, c * TILES : (c + 1) * TILES, :] = (
                share[:, c * LANES : (c + 1) * LANES] + share[:, (c + 3) * LANES : (c + 4) * LANES]
            )
        if d > 0:
            combined.append(
                send(shares.at[d], share_in.at[d - 1], share_send.at[d - 1], share_recv.at[d - 1], beside(d))
            )
    for copy in combined:
        copy.wait_recv()
    total[...] = shares[0] + share_in[0] + share_in[1] + share_in[2]
    finished = [
        send(total, total_in.at[d - 1], total_send.at[d - 1], total_recv.at[d - 1], beside(-d)) for d in (2, 1, 3)
    ]

    def lay_out(part, quarter):
        for t in range(TILES):
            lanes = pl.ds(pl.multiple_of(t * BLK + quarter * LANES, LANES), LANES)
            for c in range(3):
                out[c : c + 1, lanes] = part[c * TILES + t : c * TILES + t + 1, :]

    lay_out(total, x)
    for d, copy in zip((2, 1, 3), finished):
        copy.wait_recv()
        lay_out(total_in.at[d - 1], lax.rem(x + d, N_X))
    for copy in (*halves, *passed, *combined, *finished):
        copy.wait_send()
    wait_bytes(y_in, y_send)
    wait_bytes(y_in, coef_y_send)
    wait_bytes(z_in, z_send)
    wait_bytes(z_in, coef_z_send)


def per_device(
    positions, masses, centres, pair_halo, pair_tile, halo_slot, feedback, mixing, drive, readout
):
    dma = pltpu.SemaphoreType.DMA
    vmem = pltpu.VMEM
    args = (
        positions,
        masses.reshape(QUARTERS * TILES, LANES),
        centres.reshape(3 * HALOS // LANES, LANES),
        pair_halo,
        pair_tile,
        halo_slot,
        feedback,
        mixing,
        drive,
        readout,
    )
    share = (3 * TILES, LANES)
    return pl.pallas_call(
        kernel,
        out_shape=jax.ShapeDtypeStruct(positions.shape, F32),
        in_specs=[pl.BlockSpec(memory_space=pl.ANY)] * len(args),
        out_specs=pl.BlockSpec(memory_space=vmem),
        scratch_shapes=[
            *(vmem(a.shape, a.dtype) for a in args),
            dma((len(args),)),
            vmem((TILES, 4 * BLK), F32),
            vmem((4 * TILES, 4 * BLK), BF16),
            vmem((16, HALOS), F32),
            vmem((PAIRS, 4 * BLK), F32),
            vmem((PAIRS, LANES), F32),
            vmem((3, PAIRS, BLK), F32),
            vmem((PAIRS, BLK), jnp.int32),
            vmem((PAIRS, BLK), F32),
            vmem((2, 18 * 16, BLK), BF16),
            vmem((2, 256, BLK), BF16),
            vmem((2, 18 * 16, 256), F32),
            vmem((PAIRS, KNOTS), F32),
            vmem((2 * N_Z, PLANE, KNOTS), F32),
            vmem((N_Z, PLANE, KNOTS), F32),
            vmem((N_Z, PLANE, KNOTS), F32),
            vmem((STEPS, N_Y - 1, 2, OWNED, KNOTS), F32),
            vmem((N_Z, OWNED, KNOTS), F32),
            vmem((N_Z - 1, OWNED, KNOTS), F32),
            vmem((3, 2 * KNOTS, 2 * KNOTS), BF16),
            vmem((2 * N_Z, PLANE, KNOTS), F32),
            vmem((PAIRS, KNOTS), F32),
            vmem((PAIRS, 6 * LANES), BF16),
            vmem((N_X, *share), F32),
            vmem((N_X - 1, *share), F32),
            vmem(share, F32),
            vmem((N_X - 1, *share), F32),
            dma((STEPS,)),
            dma((STEPS,)),
            dma,
            dma((STEPS,)),
            dma,
            dma,
            dma,
            dma((len(TURNS),)),
            dma,
            dma((len(TURNS),)),
            dma((len(TURNS),)),
            dma((len(TURNS),)),
            dma((N_X - 1,)),
            dma((N_X - 1,)),
            dma((N_X - 1,)),
            dma((N_X - 1,)),
        ],
        compiler_params=pltpu.CompilerParams(
            vmem_limit_bytes=VMEM_BYTES, collective_id=0, has_side_effects=True
        ),
    )(*args)


def solution(mesh):
    return jax.shard_map(
        per_device,
        mesh=mesh,
        in_specs=(
            P(None, "space"),
            P("space"),
            P("halo", None, None),
            P("halo", "space"),
            P("halo", "space"),
            P("halo", None),
            P("halo", "space"),
            P(),
            P(),
            P(),
        ),
        out_specs=P(None, "space"),
        check_vma=False,
    )
```

```python
import jax
import jax.numpy as jnp
from jax import lax
from jax.experimental import pallas as pl
from jax.experimental.pallas import tpu as pltpu
from jax.sharding import PartitionSpec as P

BLK = 512
ITERS = 8
KNOTS = 128
TILES = 32
PAIRS = 256
HALOS = 1024
OWNED = 16
N_Y = 4
N_Z = 8
N_X = 4
PLANE = N_Y * OWNED
ROWS = N_Z * PLANE
STEPS = N_Z // 2
ORDER = (4, 3, 5, 2, 6, 1, 7, 0)
TURNS = ((7, 1), (6, 1), (4, 2), (2, 2), (0, 2))
TURNS_OF = (4, 4, 3, 3, 2, 2, 1)
PASSED = 3
LANES = 128
QUARTERS = BLK // LANES
VMEM_BYTES = 60 * 2**20
SCALE = (KNOTS - 1) / 2.6
F32 = jnp.float32
BF16 = jnp.bfloat16
MESH = pl.DeviceIdType.MESH


def two_parts(x):
    high = x.astype(BF16)
    return high, (x - high.astype(F32)).astype(BF16)


def three_parts(x):
    high = x.astype(BF16)
    rest = x - high.astype(F32)
    middle = rest.astype(BF16)
    return high, middle, (rest - middle.astype(F32)).astype(BF16)


def one_hot(mask):
    return jnp.where(mask, 1.0, 0.0).astype(BF16)


def matmul(a, b):
    return jnp.dot(a, b, preferred_element_type=F32)


def kernel(
    pos_in, mass_in, centre_in, halo_in, tile_in, slot_in, feedback_in, mixing_in, drive_in, readout_in,
    out,
    pos, mass, centre, halo, tile, slot, feedback, mixing, drive, readout, loaded,
    raw, parts, lookup, gathered, columns, offset, knot, fraction, left, right, product, pair_rows,
    dense, half_in, sums, y_in, z_sums, z_in, weights, table, coef_rows, moved, shares, share_in, total, total_in,
    half_send, half_recv, y_send, y_recv, z_send, z_recv,
    coef_z_send, coef_z_recv, coef_y_send, coef_y_recv, coef_both_send, coef_both_recv, pass_send, pass_recv,
    share_send, share_recv, total_send, total_recv,
):
    inputs = (pos_in, mass_in, centre_in, halo_in, tile_in, slot_in, feedback_in, mixing_in, drive_in, readout_in)
    copies_in = [
        pltpu.make_async_copy(source, target, loaded.at[i])
        for i, (source, target) in enumerate(
            zip(inputs, (pos, mass, centre, halo, tile, slot, feedback, mixing, drive, readout))
        )
    ]
    for copy in copies_in:
        copy.start()

    me = lax.axis_index("space")
    x = lax.axis_index("halo")
    core, y, z = lax.rem(me, 2), lax.rem(lax.div(me, 2), N_Y), lax.div(me, 2 * N_Y)

    def at(dz=0, dy=0, other=0):
        place = lax.rem(z + dz + N_Z, N_Z) * N_Y + lax.rem(y + dy + N_Y, N_Y)
        return {"space": place * 2 + (1 - core if other else core)}

    def beside(d):
        return {"halo": lax.rem(x + d + N_X, N_X)}

    def send(source, target, send_sem, recv_sem, device):
        copy = pltpu.make_async_remote_copy(
            src_ref=source,
            dst_ref=target,
            send_sem=send_sem,
            recv_sem=recv_sem,
            device_id=device,
            device_id_type=MESH,
        )
        copy.start()
        return copy

    def wait_bytes(ref, sem):
        pltpu.make_async_copy(ref, ref, sem).wait()

    barrier = pltpu.get_barrier_semaphore()
    partners = [at(other=1)]
    partners += [at(dy=d) for d in range(1, N_Y)]
    partners += [at(dz=d) for d in range(1, N_Z)]
    partners += [beside(d) for d in range(1, N_X)]
    for partner in partners:
        pl.semaphore_signal(barrier, inc=1, device_id=partner, device_id_type=MESH)

    for i in (2, 3, 4, 5):
        copies_in[i].wait()
    owner = lax.div(slot[...], OWNED)
    half = lax.rem(lax.rem(owner, 2) - core + 2, 2)
    far_y = lax.rem(lax.rem(lax.div(owner, 2), N_Y) - y + N_Y, N_Y)
    far_z = lax.rem(lax.div(owner, 2 * N_Y) - z + N_Z, N_Z)
    turn = jnp.where(far_z < N_Z // 2, N_Z - 1 - 2 * far_z, 2 * far_z - N_Z)
    row = half * ROWS + turn * PLANE + far_y * OWNED + lax.rem(slot[...], OWNED)
    lookup[...] = jnp.zeros_like(lookup)
    for j, part in enumerate(three_parts(centre[...])):
        part = part.astype(F32)
        for c in range(3):
            for i in range(HALOS // LANES):
                at_row = c * (HALOS // LANES) + i
                lookup[3 * j + c : 3 * j + c + 1, i * LANES : (i + 1) * LANES] = part[at_row : at_row + 1, :]
    lookup[9:10, :] = lax.div(row, 32).astype(F32)
    lookup[10:11, :] = lax.rem(row, 32).astype(F32)
    halo_is = one_hot(lax.broadcasted_iota(jnp.int32, (HALOS, PAIRS), 0) == halo[...])
    found = matmul(lookup[...].astype(BF16), halo_is)
    pair_row = found[9:10] * 32.0 + found[10:11]
    by_pair = jnp.concatenate(
        [
            found[0:3] + found[3:6] + found[6:9],
            pair_row,
            tile[...].astype(F32),
            jnp.zeros((LANES - 5, PAIRS), F32),
        ],
        axis=0,
    )
    columns[...] = by_pair.T

    for i in (0, 1):
        copies_in[i].wait()
    for t in range(TILES):
        for c in range(3):
            raw[t : t + 1, c * BLK : (c + 1) * BLK] = pos[c : c + 1, t * BLK : (t + 1) * BLK]
    for q in range(QUARTERS):
        raw[:, 3 * BLK + q * LANES : 3 * BLK + (q + 1) * LANES] = mass[pl.ds(q, TILES, stride=QUARTERS), :]
    for j, part in enumerate(three_parts(raw[...])):
        parts[j * TILES : (j + 1) * TILES, :] = part
    parts[3 * TILES :, :] = jnp.zeros((TILES, 4 * BLK), BF16)
    lane = lax.broadcasted_iota(jnp.int32, (PAIRS, LANES), 1)
    tile_is = one_hot((lax.rem(lane, TILES).astype(F32) == columns[:, 4:5]) & (lane < 3 * TILES))
    gathered[...] = matmul(tile_is, parts[...])

    lane8 = lax.broadcasted_iota(jnp.int32, (8, LANES), 1)
    sub8 = lax.broadcasted_iota(jnp.int32, (8, LANES), 0)
    low_lane = lax.rem(lane8, 16)

    def build(start, u):
        rows = pl.ds(pl.multiple_of(start, 16), 16)
        square = jnp.zeros((16, BLK), F32)
        for c in range(3):
            part = gathered[rows, c * BLK : (c + 1) * BLK] - columns[rows, c : c + 1]
            offset[c, rows, :] = part
            square += part * part
        scaled = jnp.sqrt(square) * SCALE
        below = jnp.floor(scaled)
        rest = scaled - below
        knot[rows, :] = below.astype(jnp.int32)
        fraction[rows, :] = rest
        coarse = jnp.floor(below * 0.125)
        fine = (below - 8.0 * coarse).astype(BF16)
        coarse = coarse.astype(BF16)
        weight = gathered[rows, 3 * BLK :]
        above = weight * rest
        w_below, w_above = two_parts(weight - above), two_parts(above)
        nothing, one = jnp.zeros((16, BLK), BF16), jnp.ones((16, BLK), BF16)
        masks = [fine == jnp.asarray(h, BF16) for h in range(8)]
        for j in range(2):
            for h in range(9):
                value = jnp.where(masks[h - 1], w_above[j], nothing) if h > 0 else nothing
                if h < 8:
                    value = jnp.where(masks[h], w_below[j], value)
                spot = (j * 9 + h) * 16
                left[u, spot : spot + 16, :] = value
        for j in range(16):
            number = (j % 8) * 2 + j // 8
            right[u, j * 16 : j * 16 + 16, :] = jnp.where(coarse == jnp.asarray(number, BF16), one, nothing)

    def fold(start, u):
        for e in range(2):
            source = (lane8 - low_lane) + sub8 + 8 * e
            profile = jnp.zeros((8, LANES), F32)
            for v in range(2):
                for h in range(9):
                    spot = h * 16 + 8 * e
                    both = (
                        product[u, spot : spot + 8, v * LANES : (v + 1) * LANES]
                        + product[u, 144 + spot : 144 + spot + 8, v * LANES : (v + 1) * LANES]
                    )
                    own = jnp.take_along_axis(both, source, axis=1)
                    to = 8 * v + h
                    if to == 16:
                        own = pltpu.roll(own, 16, 1)
                    profile += jnp.where(low_lane == to % 16, own, 0.0)
            pair_rows[pl.ds(pl.multiple_of(start + 8 * e, 8), 8), :] = profile

    def block(b, carry):
        for u in range(2):
            build(b * 32 + u * 16, u)
        for u in range(2):
            product[u] = lax.dot_general(
                left[u], right[u], (((1,), (1,)), ((), ())), preferred_element_type=F32
            )
        for u in range(2):
            fold(b * 32 + u * 16, u)
        return carry

    lax.fori_loop(0, PAIRS // 32, block, 0, unroll=8)

    row_is = one_hot(lax.broadcasted_iota(jnp.int32, (HALOS, PAIRS), 0) == pair_row.astype(jnp.int32))
    both = matmul(row_is, jnp.concatenate(two_parts(pair_rows[...]), axis=1))
    dense[...] = (both[:, :KNOTS] + both[:, KNOTS:]).reshape(2 * N_Z, PLANE, KNOTS)

    pl.semaphore_wait(barrier, len(partners))
    halves = [
        send(
            dense.at[pl.ds(N_Z + 2 * j, 2)],
            half_in.at[pl.ds(2 * j, 2)],
            half_send.at[j],
            half_recv.at[j],
            at(other=1),
        )
        for j in range(STEPS)
    ]
    for i in (6, 7, 8, 9):
        copies_in[i].wait()
    for c in range(3):
        high, low = two_parts(mixing[c])
        weights[c, :KNOTS, :KNOTS] = high
        weights[c, KNOTS:, :KNOTS] = high
        weights[c, :KNOTS, KNOTS:] = low
        weights[c, KNOTS:, KNOTS:] = low
    eye = lax.broadcasted_iota(jnp.int32, (OWNED, OWNED), 0) == lax.broadcasted_iota(
        jnp.int32, (OWNED, OWNED), 1
    )
    phi = jnp.sum(jnp.where(eye, feedback[...], 0.0), axis=1, keepdims=True)

    for j in range(STEPS):
        halves[j].wait_recv()
        turns = pl.ds(2 * j, 2)
        sums[turns] = dense[turns] + half_in[turns]
        for d in (2, 1, 3):
            send(
                sums.at[turns, pl.ds(d * OWNED, OWNED)],
                y_in.at[j, d - 1],
                y_send,
                y_recv.at[j],
                at(dy=d),
            )
    for j in range(STEPS):
        wait_bytes(y_in.at[j], y_recv.at[j])
        plane = sums[2 * j : 2 * j + 2, :OWNED] + y_in[j, 0] + y_in[j, 1] + y_in[j, 2]
        z_sums[2 * j : 2 * j + 2] = plane
        for i in (2 * j, 2 * j + 1):
            if ORDER[i]:
                send(z_sums.at[i], z_in.at[i], z_send, z_recv, at(dz=ORDER[i]))
    wait_bytes(z_in, z_recv)
    owned = z_sums[N_Z - 1]
    for i in range(N_Z - 1):
        owned += z_in[i]

    level = jnp.log1p(owned)
    driven = [drive[c : c + 1, :] * level for c in range(3)]
    state = [jnp.tanh(v) for v in driven]
    for _ in range(ITERS - 1):
        mean = (state[0] + state[1] + state[2]) * (0.5 / 3.0)
        fresh = []
        for c in range(3):
            mixed = matmul(jnp.concatenate(two_parts(state[c]), axis=1), weights[c])
            mixed = mixed[:, :KNOTS] + mixed[:, KNOTS:]
            fresh.append(jnp.tanh(driven[c] + phi * mixed + mean))
        state = fresh
    table[N_Z - 1, :OWNED] = (
        readout[0:1, :] * state[0] + readout[1:2, :] * state[1] + readout[2:3, :] * state[2]
    )

    own = table.at[N_Z - 1, pl.ds(0, OWNED)]
    for i in reversed(range(N_Z - 1)):
        send(own, table.at[i, pl.ds(0, OWNED)], coef_z_send, coef_z_recv.at[TURNS_OF[i]], at(dz=-ORDER[i]))
    passed = []
    for g, (first, count) in enumerate(TURNS):
        line = table.at[pl.ds(first, count), pl.ds(0, OWNED)]
        if g > 0:
            wait_bytes(line, coef_z_recv.at[g])
        for d in (2, 1, 3):
            send(
                line,
                table.at[pl.ds(first, count), pl.ds(d * OWNED, OWNED)],
                coef_y_send,
                coef_y_recv.at[g],
                at(dy=-d),
            )
        if g >= PASSED:
            for d in (2, 1, 3):
                send(
                    line,
                    table.at[pl.ds(N_Z + first, count), pl.ds(d * OWNED, OWNED)],
                    coef_both_send,
                    coef_both_recv.at[g - PASSED],
                    at(dy=-d, other=1),
                )
            passed.append(
                send(
                    line,
                    table.at[pl.ds(N_Z + first, count), pl.ds(0, OWNED)],
                    pass_send.at[g],
                    pass_recv.at[g],
                    at(other=1),
                )
            )
    for g, (first, count) in enumerate(TURNS):
        wait_bytes(table.at[pl.ds(first, count), pl.ds(OWNED, 3 * OWNED)], coef_y_recv.at[g])
        if g < PASSED:
            passed.append(
                send(
                    table.at[pl.ds(first, count)],
                    table.at[pl.ds(N_Z + first, count)],
                    pass_send.at[g],
                    pass_recv.at[g],
                    at(other=1),
                )
            )

    def coefficients(first):
        rows_of = lax.broadcasted_iota(jnp.int32, (PAIRS, ROWS), 1).astype(F32) + first * float(ROWS)
        rows = table[first * N_Z : (first + 1) * N_Z].reshape(ROWS, KNOTS)
        both = matmul(one_hot(rows_of == columns[:, 3:4]), jnp.concatenate(two_parts(rows), axis=1))
        return both[:, :KNOTS] + both[:, KNOTS:]

    coef_rows[...] = coefficients(0)
    tile_is = one_hot(lax.broadcasted_iota(jnp.int32, (TILES, PAIRS), 0) == tile[...])
    for copy in passed:
        copy.wait_recv()
    for g, (first, count) in enumerate(TURNS[PASSED:]):
        wait_bytes(table.at[pl.ds(N_Z + first, count), pl.ds(OWNED, 3 * OWNED)], coef_both_recv.at[g])
    coef_rows[...] += coefficients(1)

    combined = []
    for d in (2, 1, 3, 0):
        lanes = pl.ds(pl.multiple_of(lax.rem(x + d, N_X) * LANES, LANES), LANES)

        def evaluate(b, carry):
            rows = pl.ds(pl.multiple_of(b * 16, 16), 16)
            coef = coef_rows[rows, :]
            step = pltpu.roll(coef, KNOTS - 1, 1) - coef
            index = knot[rows, lanes]
            scalar = jnp.take_along_axis(coef, index, axis=1) + fraction[
                rows, lanes
            ] * jnp.take_along_axis(step, index, axis=1)
            for c in range(3):
                high, low = two_parts(offset[c, rows, lanes] * scalar)
                moved[rows, c * LANES : (c + 1) * LANES] = high
                moved[rows, (c + 3) * LANES : (c + 4) * LANES] = low
            return carry

        lax.fori_loop(0, PAIRS // 16, evaluate, 0, unroll=4)
        share = matmul(tile_is, moved[...])
        for c in range(3):
            shares[d, c * TILES : (c + 1) * TILES, :] = (
                share[:, c * LANES : (c + 1) * LANES] + share[:, (c + 3) * LANES : (c + 4) * LANES]
            )
        if d > 0:
            combined.append(
                send(shares.at[d], share_in.at[d - 1], share_send.at[d - 1], share_recv.at[d - 1], beside(d))
            )
    for copy in combined:
        copy.wait_recv()
    total[...] = shares[0] + share_in[0] + share_in[1] + share_in[2]
    finished = [
        send(total, total_in.at[d - 1], total_send.at[d - 1], total_recv.at[d - 1], beside(-d)) for d in (2, 1, 3)
    ]

    def lay_out(part, quarter):
        for t in range(TILES):
            lanes = pl.ds(pl.multiple_of(t * BLK + quarter * LANES, LANES), LANES)
            for c in range(3):
                out[c : c + 1, lanes] = part[c * TILES + t : c * TILES + t + 1, :]

    lay_out(total, x)
    for d, copy in zip((2, 1, 3), finished):
        copy.wait_recv()
        lay_out(total_in.at[d - 1], lax.rem(x + d, N_X))
    for copy in (*halves, *passed, *combined, *finished):
        copy.wait_send()
    wait_bytes(y_in, y_send)
    wait_bytes(y_in, coef_y_send)
    wait_bytes(table.at[pl.ds(0, 4), pl.ds(OWNED, 3 * OWNED)], coef_both_send)
    wait_bytes(z_in, z_send)
    wait_bytes(z_in, coef_z_send)


def per_device(
    positions, masses, centres, pair_halo, pair_tile, halo_slot, feedback, mixing, drive, readout
):
    dma = pltpu.SemaphoreType.DMA
    vmem = pltpu.VMEM
    args = (
        positions,
        masses.reshape(QUARTERS * TILES, LANES),
        centres.reshape(3 * HALOS // LANES, LANES),
        pair_halo,
        pair_tile,
        halo_slot,
        feedback,
        mixing,
        drive,
        readout,
    )
    share = (3 * TILES, LANES)
    return pl.pallas_call(
        kernel,
        out_shape=jax.ShapeDtypeStruct(positions.shape, F32),
        in_specs=[pl.BlockSpec(memory_space=pl.ANY)] * len(args),
        out_specs=pl.BlockSpec(memory_space=vmem),
        scratch_shapes=[
            *(vmem(a.shape, a.dtype) for a in args),
            dma((len(args),)),
            vmem((TILES, 4 * BLK), F32),
            vmem((4 * TILES, 4 * BLK), BF16),
            vmem((16, HALOS), F32),
            vmem((PAIRS, 4 * BLK), F32),
            vmem((PAIRS, LANES), F32),
            vmem((3, PAIRS, BLK), F32),
            vmem((PAIRS, BLK), jnp.int32),
            vmem((PAIRS, BLK), F32),
            vmem((2, 18 * 16, BLK), BF16),
            vmem((2, 256, BLK), BF16),
            vmem((2, 18 * 16, 256), F32),
            vmem((PAIRS, KNOTS), F32),
            vmem((2 * N_Z, PLANE, KNOTS), F32),
            vmem((N_Z, PLANE, KNOTS), F32),
            vmem((N_Z, PLANE, KNOTS), F32),
            vmem((STEPS, N_Y - 1, 2, OWNED, KNOTS), F32),
            vmem((N_Z, OWNED, KNOTS), F32),
            vmem((N_Z - 1, OWNED, KNOTS), F32),
            vmem((3, 2 * KNOTS, 2 * KNOTS), BF16),
            vmem((2 * N_Z, PLANE, KNOTS), F32),
            vmem((PAIRS, KNOTS), F32),
            vmem((PAIRS, 6 * LANES), BF16),
            vmem((N_X, *share), F32),
            vmem((N_X - 1, *share), F32),
            vmem(share, F32),
            vmem((N_X - 1, *share), F32),
            dma((STEPS,)),
            dma((STEPS,)),
            dma,
            dma((STEPS,)),
            dma,
            dma,
            dma,
            dma((len(TURNS),)),
            dma,
            dma((len(TURNS),)),
            dma,
            dma((len(TURNS) - PASSED,)),
            dma((len(TURNS),)),
            dma((len(TURNS),)),
            dma((N_X - 1,)),
            dma((N_X - 1,)),
            dma((N_X - 1,)),
            dma((N_X - 1,)),
        ],
        compiler_params=pltpu.CompilerParams(
            vmem_limit_bytes=VMEM_BYTES, collective_id=0, has_side_effects=True
        ),
    )(*args)


def solution(mesh):
    return jax.shard_map(
        per_device,
        mesh=mesh,
        in_specs=(
            P(None, "space"),
            P("space"),
            P("halo", None, None),
            P("halo", "space"),
            P("halo", "space"),
            P("halo", None),
            P("halo", "space"),
            P(),
            P(),
            P(),
        ),
        out_specs=P(None, "space"),
        check_vma=False,
    )
```

```python
import jax
import jax.numpy as jnp
from jax import lax
from jax.experimental import pallas as pl
from jax.experimental.pallas import tpu as pltpu
from jax.sharding import PartitionSpec as P

BLK = 512
ITERS = 8
KNOTS = 128
TILES = 32
PAIRS = 256
HALOS = 1024
OWNED = 16
N_Y = 4
N_Z = 8
N_X = 4
PLANE = N_Y * OWNED
ROWS = N_Z * PLANE
STEPS = N_Z // 2
ORDER = (4, 3, 5, 2, 6, 1, 7, 0)
TURNS = ((7, 1), (6, 1), (4, 2), (2, 2), (0, 2))
TURNS_OF = (4, 4, 3, 3, 2, 2, 1)
PASSED = 3
DIRECT = 1
LANES = 128
QUARTERS = BLK // LANES
PARTS = 2
PART = 3 * TILES // PARTS
VMEM_BYTES = 60 * 2**20
SCALE = (KNOTS - 1) / 2.6
F32 = jnp.float32
BF16 = jnp.bfloat16
MESH = pl.DeviceIdType.MESH


def two_parts(x):
    high = x.astype(BF16)
    return high, (x - high.astype(F32)).astype(BF16)


def three_parts(x):
    high = x.astype(BF16)
    rest = x - high.astype(F32)
    middle = rest.astype(BF16)
    return high, middle, (rest - middle.astype(F32)).astype(BF16)


def one_hot(mask):
    return jnp.where(mask, 1.0, 0.0).astype(BF16)


def matmul(a, b):
    return jnp.dot(a, b, preferred_element_type=F32)


def kernel(
    pos_in, mass_in, centre_in, halo_in, tile_in, slot_in, feedback_in, mixing_in, drive_in, readout_in,
    out,
    pos, mass, centre, halo, tile, slot, feedback, mixing, drive, readout, loaded,
    raw, parts, lookup, gathered, columns, offset, knot, fraction, left, right, product, pair_rows,
    dense, half_in, sums, y_in, y_other, z_sums, z_in, weights, table, coef_rows, moved, shares, share_in, total, total_in,
    half_send, half_recv, y_send, y_recv, other_send, other_recv, z_send, z_recv,
    coef_z_send, coef_z_recv, coef_y_send, coef_y_recv, coef_both_send, coef_both_recv, pass_send, pass_recv,
    share_send, share_recv, total_send, total_recv,
):
    inputs = (pos_in, mass_in, centre_in, halo_in, tile_in, slot_in, feedback_in, mixing_in, drive_in, readout_in)
    copies_in = [
        pltpu.make_async_copy(source, target, loaded.at[i])
        for i, (source, target) in enumerate(
            zip(inputs, (pos, mass, centre, halo, tile, slot, feedback, mixing, drive, readout))
        )
    ]
    for copy in copies_in:
        copy.start()

    me = lax.axis_index("space")
    x = lax.axis_index("halo")
    core, y, z = lax.rem(me, 2), lax.rem(lax.div(me, 2), N_Y), lax.div(me, 2 * N_Y)

    def at(dz=0, dy=0, other=0):
        place = lax.rem(z + dz + N_Z, N_Z) * N_Y + lax.rem(y + dy + N_Y, N_Y)
        return {"space": place * 2 + (1 - core if other else core)}

    def beside(d):
        return {"halo": lax.rem(x + d + N_X, N_X)}

    def send(source, target, send_sem, recv_sem, device):
        copy = pltpu.make_async_remote_copy(
            src_ref=source,
            dst_ref=target,
            send_sem=send_sem,
            recv_sem=recv_sem,
            device_id=device,
            device_id_type=MESH,
        )
        copy.start()
        return copy

    def wait_bytes(ref, sem):
        pltpu.make_async_copy(ref, ref, sem).wait()

    barrier = pltpu.get_barrier_semaphore()
    partners = [at(other=1)]
    partners += [at(dy=d, other=o) for d in range(1, N_Y) for o in range(2)]
    partners += [at(dz=d) for d in range(1, N_Z)]
    partners += [beside(d) for d in range(1, N_X)]
    for partner in partners:
        pl.semaphore_signal(barrier, inc=1, device_id=partner, device_id_type=MESH)

    for i in range(6):
        copies_in[i].wait()
    owner = lax.div(slot[...], OWNED)
    half = lax.rem(lax.rem(owner, 2) - core + 2, 2)
    far_y = lax.rem(lax.rem(lax.div(owner, 2), N_Y) - y + N_Y, N_Y)
    far_z = lax.rem(lax.div(owner, 2 * N_Y) - z + N_Z, N_Z)
    turn = jnp.where(far_z < N_Z // 2, N_Z - 1 - 2 * far_z, 2 * far_z - N_Z)
    row = half * ROWS + turn * PLANE + far_y * OWNED + lax.rem(slot[...], OWNED)
    lookup[...] = jnp.zeros_like(lookup)
    for j, part in enumerate(three_parts(centre[...])):
        part = part.astype(F32)
        for c in range(3):
            for i in range(HALOS // LANES):
                at_row = c * (HALOS // LANES) + i
                lookup[3 * j + c : 3 * j + c + 1, i * LANES : (i + 1) * LANES] = part[at_row : at_row + 1, :]
    lookup[9:10, :] = lax.div(row, 32).astype(F32)
    lookup[10:11, :] = lax.rem(row, 32).astype(F32)
    halo_is = one_hot(lax.broadcasted_iota(jnp.int32, (HALOS, PAIRS), 0) == halo[...])
    found = matmul(lookup[...].astype(BF16), halo_is)
    pair_row = found[9:10] * 32.0 + found[10:11]
    by_pair = jnp.concatenate(
        [
            found[0:3] + found[3:6] + found[6:9],
            pair_row,
            tile[...].astype(F32),
            jnp.zeros((LANES - 5, PAIRS), F32),
        ],
        axis=0,
    )
    columns[...] = by_pair.T

    for t in range(TILES):
        for c in range(3):
            raw[t : t + 1, c * BLK : (c + 1) * BLK] = pos[c : c + 1, t * BLK : (t + 1) * BLK]
    for q in range(QUARTERS):
        raw[:, 3 * BLK + q * LANES : 3 * BLK + (q + 1) * LANES] = mass[pl.ds(q, TILES, stride=QUARTERS), :]
    for j, part in enumerate(three_parts(raw[...])):
        parts[j * TILES : (j + 1) * TILES, :] = part
    parts[3 * TILES :, :] = jnp.zeros((TILES, 4 * BLK), BF16)
    lane = lax.broadcasted_iota(jnp.int32, (PAIRS, LANES), 1)
    tile_is = one_hot((lax.rem(lane, TILES).astype(F32) == columns[:, 4:5]) & (lane < 3 * TILES))
    gathered[...] = matmul(tile_is, parts[...])

    lane8 = lax.broadcasted_iota(jnp.int32, (8, LANES), 1)
    sub8 = lax.broadcasted_iota(jnp.int32, (8, LANES), 0)
    low_lane = lax.rem(lane8, 16)

    def build(start, u):
        rows = pl.ds(pl.multiple_of(start, 16), 16)
        square = jnp.zeros((16, BLK), F32)
        for c in range(3):
            part = gathered[rows, c * BLK : (c + 1) * BLK] - columns[rows, c : c + 1]
            offset[c, rows, :] = part
            square += part * part
        scaled = jnp.sqrt(square) * SCALE
        below = jnp.floor(scaled)
        rest = scaled - below
        knot[rows, :] = below.astype(jnp.int32)
        fraction[rows, :] = rest
        coarse = jnp.floor(below * 0.125)
        fine = (below - 8.0 * coarse).astype(BF16)
        coarse = coarse.astype(BF16)
        weight = gathered[rows, 3 * BLK :]
        above = weight * rest
        w_below, w_above = two_parts(weight - above), two_parts(above)
        nothing, one = jnp.zeros((16, BLK), BF16), jnp.ones((16, BLK), BF16)
        masks = [fine == jnp.asarray(h, BF16) for h in range(8)]
        for j in range(2):
            for h in range(9):
                value = jnp.where(masks[h - 1], w_above[j], nothing) if h > 0 else nothing
                if h < 8:
                    value = jnp.where(masks[h], w_below[j], value)
                spot = (j * 9 + h) * 16
                left[u, spot : spot + 16, :] = value
        for j in range(16):
            number = (j % 8) * 2 + j // 8
            right[u, j * 16 : j * 16 + 16, :] = jnp.where(coarse == jnp.asarray(number, BF16), one, nothing)

    def fold(start, u):
        for e in range(2):
            source = (lane8 - low_lane) + sub8 + 8 * e
            profile = jnp.zeros((8, LANES), F32)
            for v in range(2):
                for h in range(9):
                    spot = h * 16 + 8 * e
                    both = (
                        product[u, spot : spot + 8, v * LANES : (v + 1) * LANES]
                        + product[u, 144 + spot : 144 + spot + 8, v * LANES : (v + 1) * LANES]
                    )
                    own = jnp.take_along_axis(both, source, axis=1)
                    to = 8 * v + h
                    if to == 16:
                        own = pltpu.roll(own, 16, 1)
                    profile += jnp.where(low_lane == to % 16, own, 0.0)
            pair_rows[pl.ds(pl.multiple_of(start + 8 * e, 8), 8), :] = profile

    def block(b, carry):
        for u in range(2):
            build(b * 32 + u * 16, u)
        for u in range(2):
            product[u] = lax.dot_general(
                left[u], right[u], (((1,), (1,)), ((), ())), preferred_element_type=F32
            )
        for u in range(2):
            fold(b * 32 + u * 16, u)
        return carry

    lax.fori_loop(0, PAIRS // 32, block, 0, unroll=8)

    profiles = jnp.concatenate(two_parts(pair_rows[...]), axis=1)

    def sum_rows(first, count):
        rows_of = lax.broadcasted_iota(jnp.int32, (count * PLANE, PAIRS), 0) + first * PLANE
        both = matmul(one_hot(rows_of == pair_row.astype(jnp.int32)), profiles)
        dense[first : first + count] = (both[:, :KNOTS] + both[:, KNOTS:]).reshape(count, PLANE, KNOTS)

    sum_rows(0, 2 * DIRECT)
    sum_rows(N_Z, 2 * DIRECT)

    pl.semaphore_wait(barrier, len(partners))
    for j in range(DIRECT):
        for d in (2, 1, 3):
            rows = pl.ds(d * OWNED, OWNED)
            send(dense.at[pl.ds(2 * j, 2), rows], y_in.at[j, d - 1], y_send, y_recv.at[j], at(dy=d))
            send(
                dense.at[pl.ds(N_Z + 2 * j, 2), rows],
                y_other.at[j, d - 1],
                other_send,
                other_recv.at[j],
                at(dy=d, other=1),
            )
    sum_rows(N_Z + 2 * DIRECT, N_Z - 2 * DIRECT)
    halves = []
    for j in range(STEPS):
        rows = pl.ds(0, OWNED if j < DIRECT else PLANE)
        halves.append(
            send(
                dense.at[pl.ds(N_Z + 2 * j, 2), rows],
                half_in.at[pl.ds(2 * j, 2), rows],
                half_send.at[j],
                half_recv.at[j],
                at(other=1),
            )
        )
    sum_rows(2 * DIRECT, N_Z - 2 * DIRECT)
    for i in (6, 7, 8, 9):
        copies_in[i].wait()
    for c in range(3):
        high, low = two_parts(mixing[c])
        weights[c, :KNOTS, :KNOTS] = high
        weights[c, KNOTS:, :KNOTS] = high
        weights[c, :KNOTS, KNOTS:] = low
        weights[c, KNOTS:, KNOTS:] = low
    eye = lax.broadcasted_iota(jnp.int32, (OWNED, OWNED), 0) == lax.broadcasted_iota(
        jnp.int32, (OWNED, OWNED), 1
    )
    phi = jnp.sum(jnp.where(eye, feedback[...], 0.0), axis=1, keepdims=True)

    for j in range(DIRECT, STEPS):
        halves[j].wait_recv()
        turns = pl.ds(2 * j, 2)
        sums[turns] = dense[turns] + half_in[turns]
        for d in (2, 1, 3):
            send(
                sums.at[turns, pl.ds(d * OWNED, OWNED)],
                y_in.at[j, d - 1],
                y_send,
                y_recv.at[j],
                at(dy=d),
            )
    for j in range(STEPS):
        turns = slice(2 * j, 2 * j + 2)
        if j < DIRECT:
            halves[j].wait_recv()
            wait_bytes(y_other.at[j], other_recv.at[j])
            plane = dense[turns, :OWNED] + half_in[turns, :OWNED] + y_other[j, 0] + y_other[j, 1] + y_other[j, 2]
        else:
            plane = sums[turns, :OWNED]
        wait_bytes(y_in.at[j], y_recv.at[j])
        plane += y_in[j, 0] + y_in[j, 1] + y_in[j, 2]
        z_sums[2 * j : 2 * j + 2] = plane
        for i in (2 * j, 2 * j + 1):
            if ORDER[i]:
                send(z_sums.at[i], z_in.at[i], z_send, z_recv, at(dz=ORDER[i]))
    wait_bytes(z_in, z_recv)
    owned = z_sums[N_Z - 1]
    for i in range(N_Z - 1):
        owned += z_in[i]

    level = jnp.log1p(owned)
    driven = [drive[c : c + 1, :] * level for c in range(3)]
    state = [jnp.tanh(v) for v in driven]
    for _ in range(ITERS - 1):
        mean = (state[0] + state[1] + state[2]) * (0.5 / 3.0)
        fresh = []
        for c in range(3):
            mixed = matmul(jnp.concatenate(two_parts(state[c]), axis=1), weights[c])
            mixed = mixed[:, :KNOTS] + mixed[:, KNOTS:]
            fresh.append(jnp.tanh(driven[c] + phi * mixed + mean))
        state = fresh
    table[N_Z - 1, :OWNED] = (
        readout[0:1, :] * state[0] + readout[1:2, :] * state[1] + readout[2:3, :] * state[2]
    )

    own = table.at[N_Z - 1, pl.ds(0, OWNED)]
    for i in reversed(range(N_Z - 1)):
        send(own, table.at[i, pl.ds(0, OWNED)], coef_z_send, coef_z_recv.at[TURNS_OF[i]], at(dz=-ORDER[i]))
    passed = []
    for g, (first, count) in enumerate(TURNS):
        line = table.at[pl.ds(first, count), pl.ds(0, OWNED)]
        if g > 0:
            wait_bytes(line, coef_z_recv.at[g])
        for d in (2, 1, 3):
            send(
                line,
                table.at[pl.ds(first, count), pl.ds(d * OWNED, OWNED)],
                coef_y_send,
                coef_y_recv.at[g],
                at(dy=-d),
            )
        if g >= PASSED:
            for d in (2, 1, 3):
                send(
                    line,
                    table.at[pl.ds(N_Z + first, count), pl.ds(d * OWNED, OWNED)],
                    coef_both_send,
                    coef_both_recv.at[g - PASSED],
                    at(dy=-d, other=1),
                )
            passed.append(
                send(
                    line,
                    table.at[pl.ds(N_Z + first, count), pl.ds(0, OWNED)],
                    pass_send.at[g],
                    pass_recv.at[g],
                    at(other=1),
                )
            )
    for g, (first, count) in enumerate(TURNS):
        wait_bytes(table.at[pl.ds(first, count), pl.ds(OWNED, 3 * OWNED)], coef_y_recv.at[g])
        if g < PASSED:
            passed.append(
                send(
                    table.at[pl.ds(first, count)],
                    table.at[pl.ds(N_Z + first, count)],
                    pass_send.at[g],
                    pass_recv.at[g],
                    at(other=1),
                )
            )

    def coefficients(first):
        rows_of = lax.broadcasted_iota(jnp.int32, (PAIRS, ROWS), 1).astype(F32) + first * float(ROWS)
        rows = table[first * N_Z : (first + 1) * N_Z].reshape(ROWS, KNOTS)
        both = matmul(one_hot(rows_of == columns[:, 3:4]), jnp.concatenate(two_parts(rows), axis=1))
        return both[:, :KNOTS] + both[:, KNOTS:]

    coef_rows[...] = coefficients(0)
    tile_is = one_hot(lax.broadcasted_iota(jnp.int32, (TILES, PAIRS), 0) == tile[...])
    for copy in passed:
        copy.wait_recv()
    for g, (first, count) in enumerate(TURNS[PASSED:]):
        wait_bytes(table.at[pl.ds(N_Z + first, count), pl.ds(OWNED, 3 * OWNED)], coef_both_recv.at[g])
    coef_rows[...] += coefficients(1)

    combined = []
    for d in (2, 1, 3, 0):
        lanes = pl.ds(pl.multiple_of(lax.rem(x + d, N_X) * LANES, LANES), LANES)

        def evaluate(b, carry):
            rows = pl.ds(pl.multiple_of(b * 16, 16), 16)
            coef = coef_rows[rows, :]
            step = pltpu.roll(coef, KNOTS - 1, 1) - coef
            index = knot[rows, lanes]
            scalar = jnp.take_along_axis(coef, index, axis=1) + fraction[
                rows, lanes
            ] * jnp.take_along_axis(step, index, axis=1)
            for c in range(3):
                high, low = two_parts(offset[c, rows, lanes] * scalar)
                moved[rows, c * LANES : (c + 1) * LANES] = high
                moved[rows, (c + 3) * LANES : (c + 4) * LANES] = low
            return carry

        lax.fori_loop(0, PAIRS // 16, evaluate, 0, unroll=8)
        share = matmul(tile_is, moved[...])
        for c in range(3):
            shares[d, c * TILES : (c + 1) * TILES, :] = (
                share[:, c * LANES : (c + 1) * LANES] + share[:, (c + 3) * LANES : (c + 4) * LANES]
            )
        if d > 0:
            for part in range(PARTS):
                rows = pl.ds(part * PART, PART)
                combined.append(
                    send(
                        shares.at[d, rows],
                        share_in.at[d - 1, rows],
                        share_send.at[part, d - 1],
                        share_recv.at[part, d - 1],
                        beside(d),
                    )
                )
    finished = []
    for part in range(PARTS):
        for copy in combined[part::PARTS]:
            copy.wait_recv()
        rows = pl.ds(part * PART, PART)
        total[rows, :] = shares[0, rows] + share_in[0, rows] + share_in[1, rows] + share_in[2, rows]
        for d in (2, 1, 3):
            finished.append(
                send(
                    total.at[rows],
                    total_in.at[d - 1, rows],
                    total_send.at[part, d - 1],
                    total_recv.at[part, d - 1],
                    beside(-d),
                )
            )

    def lay_out(part, quarter):
        for t in range(TILES):
            lanes = pl.ds(pl.multiple_of(t * BLK + quarter * LANES, LANES), LANES)
            for c in range(3):
                out[c : c + 1, lanes] = part[c * TILES + t : c * TILES + t + 1, :]

    lay_out(total, x)
    for i, d in ((1, 1), (2, 3), (0, 2)):
        for part in range(PARTS):
            finished[3 * part + i].wait_recv()
        lay_out(total_in.at[d - 1], lax.rem(x + d, N_X))
    for copy in (*halves, *passed, *combined, *finished):
        copy.wait_send()
    wait_bytes(y_in, y_send)
    wait_bytes(y_other, other_send)
    wait_bytes(y_in, coef_y_send)
    wait_bytes(table.at[pl.ds(0, 4), pl.ds(OWNED, 3 * OWNED)], coef_both_send)
    wait_bytes(z_in, z_send)
    wait_bytes(z_in, coef_z_send)


def per_device(
    positions, masses, centres, pair_halo, pair_tile, halo_slot, feedback, mixing, drive, readout
):
    dma = pltpu.SemaphoreType.DMA
    vmem = pltpu.VMEM
    args = (
        positions,
        masses.reshape(QUARTERS * TILES, LANES),
        centres.reshape(3 * HALOS // LANES, LANES),
        pair_halo,
        pair_tile,
        halo_slot,
        feedback,
        mixing,
        drive,
        readout,
    )
    share = (3 * TILES, LANES)
    return pl.pallas_call(
        kernel,
        out_shape=jax.ShapeDtypeStruct(positions.shape, F32),
        in_specs=[pl.BlockSpec(memory_space=pl.ANY)] * len(args),
        out_specs=pl.BlockSpec(memory_space=vmem),
        scratch_shapes=[
            *(vmem(a.shape, a.dtype) for a in args),
            dma((len(args),)),
            vmem((TILES, 4 * BLK), F32),
            vmem((4 * TILES, 4 * BLK), BF16),
            vmem((16, HALOS), F32),
            vmem((PAIRS, 4 * BLK), F32),
            vmem((PAIRS, LANES), F32),
            vmem((3, PAIRS, BLK), F32),
            vmem((PAIRS, BLK), jnp.int32),
            vmem((PAIRS, BLK), F32),
            vmem((2, 18 * 16, BLK), BF16),
            vmem((2, 256, BLK), BF16),
            vmem((2, 18 * 16, 256), F32),
            vmem((PAIRS, KNOTS), F32),
            vmem((2 * N_Z, PLANE, KNOTS), F32),
            vmem((N_Z, PLANE, KNOTS), F32),
            vmem((N_Z, PLANE, KNOTS), F32),
            vmem((STEPS, N_Y - 1, 2, OWNED, KNOTS), F32),
            vmem((DIRECT, N_Y - 1, 2, OWNED, KNOTS), F32),
            vmem((N_Z, OWNED, KNOTS), F32),
            vmem((N_Z - 1, OWNED, KNOTS), F32),
            vmem((3, 2 * KNOTS, 2 * KNOTS), BF16),
            vmem((2 * N_Z, PLANE, KNOTS), F32),
            vmem((PAIRS, KNOTS), F32),
            vmem((PAIRS, 6 * LANES), BF16),
            vmem((N_X, *share), F32),
            vmem((N_X - 1, *share), F32),
            vmem(share, F32),
            vmem((N_X - 1, *share), F32),
            dma((STEPS,)),
            dma((STEPS,)),
            dma,
            dma((STEPS,)),
            dma,
            dma((DIRECT,)),
            dma,
            dma,
            dma,
            dma((len(TURNS),)),
            dma,
            dma((len(TURNS),)),
            dma,
            dma((len(TURNS) - PASSED,)),
            dma((len(TURNS),)),
            dma((len(TURNS),)),
            dma((PARTS, N_X - 1)),
            dma((PARTS, N_X - 1)),
            dma((PARTS, N_X - 1)),
            dma((PARTS, N_X - 1)),
        ],
        compiler_params=pltpu.CompilerParams(
            vmem_limit_bytes=VMEM_BYTES, collective_id=0, has_side_effects=True
        ),
    )(*args)


def solution(mesh):
    return jax.shard_map(
        per_device,
        mesh=mesh,
        in_specs=(
            P(None, "space"),
            P("space"),
            P("halo", None, None),
            P("halo", "space"),
            P("halo", "space"),
            P("halo", None),
            P("halo", "space"),
            P(),
            P(),
            P(),
        ),
        out_specs=P(None, "space"),
        check_vma=False,
    )
```

```python
import jax
import jax.numpy as jnp
from jax import lax
from jax.experimental import pallas as pl
from jax.experimental.pallas import tpu as pltpu
from jax.sharding import PartitionSpec as P

BLK = 512
ITERS = 8
KNOTS = 128
TILES = 32
PAIRS = 256
HALOS = 1024
OWNED = 16
N_Y = 4
N_Z = 8
N_X = 4
PLANE = N_Y * OWNED
ROWS = N_Z * PLANE
STEPS = N_Z // 2
ORDER = (4, 3, 5, 2, 6, 1, 7, 0)
TURNS = ((7, 1), (6, 1), (4, 2), (2, 2), (0, 2))
TURNS_OF = (4, 4, 3, 3, 2, 2, 1)
PASSED = 3
DIRECT = 1
LANES = 128
QUARTERS = BLK // LANES
PARTS = 2
PART = 3 * TILES // PARTS
VMEM_BYTES = 60 * 2**20
SCALE = (KNOTS - 1) / 2.6
F32 = jnp.float32
BF16 = jnp.bfloat16
MESH = pl.DeviceIdType.MESH


def two_parts(x):
    high = x.astype(BF16)
    return high, (x - high.astype(F32)).astype(BF16)


def three_parts(x):
    high = x.astype(BF16)
    rest = x - high.astype(F32)
    middle = rest.astype(BF16)
    return high, middle, (rest - middle.astype(F32)).astype(BF16)


def one_hot(mask):
    return jnp.where(mask, 1.0, 0.0).astype(BF16)


def matmul(a, b):
    return jnp.dot(a, b, preferred_element_type=F32)


def kernel(
    pos_in, mass_in, centre_in, halo_in, tile_in, slot_in, feedback_in, mixing_in, drive_in, readout_in,
    out,
    pos, mass, centre, halo, tile, slot, feedback, mixing, drive, readout, loaded,
    raw, parts, lookup, gathered, columns, offset, knot, fraction, left, right, product, pair_rows,
    dense, half_in, sums, y_in, y_other, z_sums, z_in, weights, table, picked, tile_of, coef_rows, moved, shares, share_in, total, total_in,
    half_send, half_recv, y_send, y_recv, other_send, other_recv, z_send, z_recv,
    coef_z_send, coef_z_recv, coef_y_send, coef_y_recv, coef_both_send, coef_both_recv, pass_send, pass_recv,
    share_send, share_recv, total_send, total_recv,
):
    inputs = (pos_in, mass_in, centre_in, halo_in, tile_in, slot_in, feedback_in, mixing_in, drive_in, readout_in)
    copies_in = [
        pltpu.make_async_copy(source, target, loaded.at[i])
        for i, (source, target) in enumerate(
            zip(inputs, (pos, mass, centre, halo, tile, slot, feedback, mixing, drive, readout))
        )
    ]
    for copy in copies_in:
        copy.start()

    me = lax.axis_index("space")
    x = lax.axis_index("halo")
    core, y, z = lax.rem(me, 2), lax.rem(lax.div(me, 2), N_Y), lax.div(me, 2 * N_Y)

    def at(dz=0, dy=0, other=0):
        place = lax.rem(z + dz + N_Z, N_Z) * N_Y + lax.rem(y + dy + N_Y, N_Y)
        return {"space": place * 2 + (1 - core if other else core)}

    def beside(d):
        return {"halo": lax.rem(x + d + N_X, N_X)}

    def send(source, target, send_sem, recv_sem, device):
        copy = pltpu.make_async_remote_copy(
            src_ref=source,
            dst_ref=target,
            send_sem=send_sem,
            recv_sem=recv_sem,
            device_id=device,
            device_id_type=MESH,
        )
        copy.start()
        return copy

    def wait_bytes(ref, sem):
        pltpu.make_async_copy(ref, ref, sem).wait()

    barrier = pltpu.get_barrier_semaphore()
    partners = [at(other=1)]
    partners += [at(dy=d, other=o) for d in range(1, N_Y) for o in range(2)]
    partners += [at(dz=d) for d in range(1, N_Z)]
    partners += [beside(d) for d in range(1, N_X)]
    for partner in partners:
        pl.semaphore_signal(barrier, inc=1, device_id=partner, device_id_type=MESH)

    for i in range(6):
        copies_in[i].wait()
    owner = lax.div(slot[...], OWNED)
    half = lax.rem(lax.rem(owner, 2) - core + 2, 2)
    far_y = lax.rem(lax.rem(lax.div(owner, 2), N_Y) - y + N_Y, N_Y)
    far_z = lax.rem(lax.div(owner, 2 * N_Y) - z + N_Z, N_Z)
    turn = jnp.where(far_z < N_Z // 2, N_Z - 1 - 2 * far_z, 2 * far_z - N_Z)
    row = half * ROWS + turn * PLANE + far_y * OWNED + lax.rem(slot[...], OWNED)
    lookup[...] = jnp.zeros_like(lookup)
    for j, part in enumerate(three_parts(centre[...])):
        part = part.astype(F32)
        for c in range(3):
            for i in range(HALOS // LANES):
                at_row = c * (HALOS // LANES) + i
                lookup[3 * j + c : 3 * j + c + 1, i * LANES : (i + 1) * LANES] = part[at_row : at_row + 1, :]
    lookup[9:10, :] = lax.div(row, 32).astype(F32)
    lookup[10:11, :] = lax.rem(row, 32).astype(F32)
    halo_is = one_hot(lax.broadcasted_iota(jnp.int32, (HALOS, PAIRS), 0) == halo[...])
    found = matmul(lookup[...].astype(BF16), halo_is)
    pair_row = found[9:10] * 32.0 + found[10:11]
    by_pair = jnp.concatenate(
        [
            found[0:3] + found[3:6] + found[6:9],
            pair_row,
            tile[...].astype(F32),
            jnp.zeros((LANES - 5, PAIRS), F32),
        ],
        axis=0,
    )
    columns[...] = by_pair.T

    for t in range(TILES):
        for c in range(3):
            raw[t : t + 1, c * BLK : (c + 1) * BLK] = pos[c : c + 1, t * BLK : (t + 1) * BLK]
    for q in range(QUARTERS):
        raw[:, 3 * BLK + q * LANES : 3 * BLK + (q + 1) * LANES] = mass[pl.ds(q, TILES, stride=QUARTERS), :]
    for j, part in enumerate(three_parts(raw[...])):
        parts[j * TILES : (j + 1) * TILES, :] = part
    parts[3 * TILES :, :] = jnp.zeros((TILES, 4 * BLK), BF16)
    lane = lax.broadcasted_iota(jnp.int32, (PAIRS, LANES), 1)
    tile_is = one_hot((lax.rem(lane, TILES).astype(F32) == columns[:, 4:5]) & (lane < 3 * TILES))
    gathered[...] = matmul(tile_is, parts[...])

    lane8 = lax.broadcasted_iota(jnp.int32, (8, LANES), 1)
    sub8 = lax.broadcasted_iota(jnp.int32, (8, LANES), 0)
    low_lane = lax.rem(lane8, 16)

    def build(start, u):
        rows = pl.ds(pl.multiple_of(start, 16), 16)
        square = jnp.zeros((16, BLK), F32)
        for c in range(3):
            part = gathered[rows, c * BLK : (c + 1) * BLK] - columns[rows, c : c + 1]
            offset[c, rows, :] = part
            square += part * part
        scaled = jnp.sqrt(square) * SCALE
        below = jnp.floor(scaled)
        rest = scaled - below
        knot[rows, :] = below.astype(jnp.int32)
        fraction[rows, :] = rest
        coarse = jnp.floor(below * 0.125)
        fine = (below - 8.0 * coarse).astype(BF16)
        coarse = coarse.astype(BF16)
        weight = gathered[rows, 3 * BLK :]
        above = weight * rest
        w_below, w_above = two_parts(weight - above), two_parts(above)
        nothing, one = jnp.zeros((16, BLK), BF16), jnp.ones((16, BLK), BF16)
        masks = [fine == jnp.asarray(h, BF16) for h in range(8)]
        for j in range(2):
            for h in range(9):
                value = jnp.where(masks[h - 1], w_above[j], nothing) if h > 0 else nothing
                if h < 8:
                    value = jnp.where(masks[h], w_below[j], value)
                spot = (j * 9 + h) * 16
                left[u, spot : spot + 16, :] = value
        for j in range(16):
            number = (j % 8) * 2 + j // 8
            right[u, j * 16 : j * 16 + 16, :] = jnp.where(coarse == jnp.asarray(number, BF16), one, nothing)

    def fold(start, u):
        for e in range(2):
            source = (lane8 - low_lane) + sub8 + 8 * e
            profile = jnp.zeros((8, LANES), F32)
            for v in range(2):
                for h in range(9):
                    spot = h * 16 + 8 * e
                    both = (
                        product[u, spot : spot + 8, v * LANES : (v + 1) * LANES]
                        + product[u, 144 + spot : 144 + spot + 8, v * LANES : (v + 1) * LANES]
                    )
                    own = jnp.take_along_axis(both, source, axis=1)
                    to = 8 * v + h
                    if to == 16:
                        own = pltpu.roll(own, 16, 1)
                    profile += jnp.where(low_lane == to % 16, own, 0.0)
            pair_rows[pl.ds(pl.multiple_of(start + 8 * e, 8), 8), :] = profile

    def block(b, carry):
        for u in range(2):
            build(b * 32 + u * 16, u)
        for u in range(2):
            product[u] = lax.dot_general(
                left[u], right[u], (((1,), (1,)), ((), ())), preferred_element_type=F32
            )
        for u in range(2):
            fold(b * 32 + u * 16, u)
        return carry

    lax.fori_loop(0, PAIRS // 32, block, 0, unroll=8)

    profiles = jnp.concatenate(two_parts(pair_rows[...]), axis=1)

    def sum_rows(first, count):
        rows_of = lax.broadcasted_iota(jnp.int32, (count * PLANE, PAIRS), 0) + first * PLANE
        both = matmul(one_hot(rows_of == pair_row.astype(jnp.int32)), profiles)
        dense[first : first + count] = (both[:, :KNOTS] + both[:, KNOTS:]).reshape(count, PLANE, KNOTS)

    sum_rows(0, 2 * DIRECT)
    sum_rows(N_Z, 2 * DIRECT)

    pl.semaphore_wait(barrier, len(partners))
    for j in range(DIRECT):
        for d in (2, 1, 3):
            rows = pl.ds(d * OWNED, OWNED)
            send(dense.at[pl.ds(2 * j, 2), rows], y_in.at[j, d - 1], y_send, y_recv.at[j], at(dy=d))
            send(
                dense.at[pl.ds(N_Z + 2 * j, 2), rows],
                y_other.at[j, d - 1],
                other_send,
                other_recv.at[j],
                at(dy=d, other=1),
            )
    sum_rows(N_Z + 2 * DIRECT, N_Z - 2 * DIRECT)
    halves = []
    for j in range(STEPS):
        rows = pl.ds(0, OWNED if j < DIRECT else PLANE)
        halves.append(
            send(
                dense.at[pl.ds(N_Z + 2 * j, 2), rows],
                half_in.at[pl.ds(2 * j, 2), rows],
                half_send.at[j],
                half_recv.at[j],
                at(other=1),
            )
        )
    sum_rows(2 * DIRECT, N_Z - 2 * DIRECT)
    for i in (6, 7, 8, 9):
        copies_in[i].wait()
    for c in range(3):
        high, low = two_parts(mixing[c])
        weights[c, :KNOTS, :KNOTS] = high
        weights[c, KNOTS:, :KNOTS] = high
        weights[c, :KNOTS, KNOTS:] = low
        weights[c, KNOTS:, KNOTS:] = low
    eye = lax.broadcasted_iota(jnp.int32, (OWNED, OWNED), 0) == lax.broadcasted_iota(
        jnp.int32, (OWNED, OWNED), 1
    )
    phi = jnp.sum(jnp.where(eye, feedback[...], 0.0), axis=1, keepdims=True)

    rows_of = lax.broadcasted_iota(jnp.int32, (PAIRS, ROWS), 1).astype(F32)
    for first in range(2):
        picked[first] = one_hot(rows_of + first * float(ROWS) == columns[:, 3:4])
    tile_of[...] = one_hot(lax.broadcasted_iota(jnp.int32, (TILES, PAIRS), 0) == tile[...])

    for j in range(DIRECT, STEPS):
        halves[j].wait_recv()
        turns = pl.ds(2 * j, 2)
        sums[turns] = dense[turns] + half_in[turns]
        for d in (2, 1, 3):
            send(
                sums.at[turns, pl.ds(d * OWNED, OWNED)],
                y_in.at[j, d - 1],
                y_send,
                y_recv.at[j],
                at(dy=d),
            )
    for j in range(STEPS):
        turns = slice(2 * j, 2 * j + 2)
        if j < DIRECT:
            halves[j].wait_recv()
            wait_bytes(y_other.at[j], other_recv.at[j])
            plane = dense[turns, :OWNED] + half_in[turns, :OWNED] + y_other[j, 0] + y_other[j, 1] + y_other[j, 2]
        else:
            plane = sums[turns, :OWNED]
        wait_bytes(y_in.at[j], y_recv.at[j])
        plane += y_in[j, 0] + y_in[j, 1] + y_in[j, 2]
        z_sums[2 * j : 2 * j + 2] = plane
        for i in (2 * j, 2 * j + 1):
            if ORDER[i]:
                send(z_sums.at[i], z_in.at[i], z_send, z_recv, at(dz=ORDER[i]))
    wait_bytes(z_in, z_recv)
    owned = z_sums[N_Z - 1]
    for i in range(N_Z - 1):
        owned += z_in[i]

    level = jnp.log1p(owned)
    driven = [drive[c : c + 1, :] * level for c in range(3)]
    state = [jnp.tanh(v) for v in driven]
    for _ in range(ITERS - 1):
        mean = (state[0] + state[1] + state[2]) * (0.5 / 3.0)
        fresh = []
        for c in range(3):
            mixed = matmul(jnp.concatenate(two_parts(state[c]), axis=1), weights[c])
            mixed = mixed[:, :KNOTS] + mixed[:, KNOTS:]
            fresh.append(jnp.tanh(driven[c] + phi * mixed + mean))
        state = fresh
    table[N_Z - 1, :OWNED] = (
        readout[0:1, :] * state[0] + readout[1:2, :] * state[1] + readout[2:3, :] * state[2]
    )

    own = table.at[N_Z - 1, pl.ds(0, OWNED)]
    for i in range(N_Z - 1):
        send(own, table.at[i, pl.ds(0, OWNED)], coef_z_send, coef_z_recv.at[TURNS_OF[i]], at(dz=-ORDER[i]))
    passed = []
    for g, (first, count) in enumerate(TURNS):
        line = table.at[pl.ds(first, count), pl.ds(0, OWNED)]
        if g > 0:
            wait_bytes(line, coef_z_recv.at[g])
        for d in (2, 1, 3):
            send(
                line,
                table.at[pl.ds(first, count), pl.ds(d * OWNED, OWNED)],
                coef_y_send,
                coef_y_recv.at[g],
                at(dy=-d),
            )
        if g >= PASSED:
            for d in (2, 1, 3):
                send(
                    line,
                    table.at[pl.ds(N_Z + first, count), pl.ds(d * OWNED, OWNED)],
                    coef_both_send,
                    coef_both_recv.at[g - PASSED],
                    at(dy=-d, other=1),
                )
            passed.append(
                send(
                    line,
                    table.at[pl.ds(N_Z + first, count), pl.ds(0, OWNED)],
                    pass_send.at[g],
                    pass_recv.at[g],
                    at(other=1),
                )
            )
    for g, (first, count) in enumerate(TURNS):
        wait_bytes(table.at[pl.ds(first, count), pl.ds(OWNED, 3 * OWNED)], coef_y_recv.at[g])
        if g < PASSED:
            passed.append(
                send(
                    table.at[pl.ds(first, count)],
                    table.at[pl.ds(N_Z + first, count)],
                    pass_send.at[g],
                    pass_recv.at[g],
                    at(other=1),
                )
            )

    def coefficients(first):
        rows = table[first * N_Z : (first + 1) * N_Z].reshape(ROWS, KNOTS)
        both = matmul(picked[first], jnp.concatenate(two_parts(rows), axis=1))
        return both[:, :KNOTS] + both[:, KNOTS:]

    coef_rows[...] = coefficients(0)
    for copy in passed:
        copy.wait_recv()
    for g, (first, count) in enumerate(TURNS[PASSED:]):
        wait_bytes(table.at[pl.ds(N_Z + first, count), pl.ds(OWNED, 3 * OWNED)], coef_both_recv.at[g])
    coef_rows[...] += coefficients(1)

    combined = []
    for d in (2, 1, 3, 0):
        lanes = pl.ds(pl.multiple_of(lax.rem(x + d, N_X) * LANES, LANES), LANES)

        def evaluate(b, carry):
            rows = pl.ds(pl.multiple_of(b * 16, 16), 16)
            coef = coef_rows[rows, :]
            step = pltpu.roll(coef, KNOTS - 1, 1) - coef
            index = knot[rows, lanes]
            scalar = jnp.take_along_axis(coef, index, axis=1) + fraction[
                rows, lanes
            ] * jnp.take_along_axis(step, index, axis=1)
            for c in range(3):
                high, low = two_parts(offset[c, rows, lanes] * scalar)
                moved[rows, c * LANES : (c + 1) * LANES] = high
                moved[rows, (c + 3) * LANES : (c + 4) * LANES] = low
            return carry

        lax.fori_loop(0, PAIRS // 16, evaluate, 0, unroll=16)
        share = matmul(tile_of[...], moved[...])
        for c in range(3):
            shares[d, c * TILES : (c + 1) * TILES, :] = (
                share[:, c * LANES : (c + 1) * LANES] + share[:, (c + 3) * LANES : (c + 4) * LANES]
            )
        if d > 0:
            for part in range(PARTS):
                rows = pl.ds(part * PART, PART)
                combined.append(
                    send(
                        shares.at[d, rows],
                        share_in.at[d - 1, rows],
                        share_send.at[part, d - 1],
                        share_recv.at[part, d - 1],
                        beside(d),
                    )
                )
    finished = []
    for part in range(PARTS):
        for copy in combined[part::PARTS]:
            copy.wait_recv()
        rows = pl.ds(part * PART, PART)
        total[rows, :] = shares[0, rows] + share_in[0, rows] + share_in[1, rows] + share_in[2, rows]
        for d in (2, 1, 3):
            finished.append(
                send(
                    total.at[rows],
                    total_in.at[d - 1, rows],
                    total_send.at[part, d - 1],
                    total_recv.at[part, d - 1],
                    beside(-d),
                )
            )

    def lay_out(part, quarter):
        for t in range(TILES):
            lanes = pl.ds(pl.multiple_of(t * BLK + quarter * LANES, LANES), LANES)
            for c in range(3):
                out[c : c + 1, lanes] = part[c * TILES + t : c * TILES + t + 1, :]

    lay_out(total, x)
    for i, d in ((1, 1), (2, 3), (0, 2)):
        for part in range(PARTS):
            finished[3 * part + i].wait_recv()
        lay_out(total_in.at[d - 1], lax.rem(x + d, N_X))
    for copy in (*halves, *passed, *combined, *finished):
        copy.wait_send()
    wait_bytes(y_in, y_send)
    wait_bytes(y_other, other_send)
    wait_bytes(y_in, coef_y_send)
    wait_bytes(table.at[pl.ds(0, 4), pl.ds(OWNED, 3 * OWNED)], coef_both_send)
    wait_bytes(z_in, z_send)
    wait_bytes(z_in, coef_z_send)


def per_device(
    positions, masses, centres, pair_halo, pair_tile, halo_slot, feedback, mixing, drive, readout
):
    dma = pltpu.SemaphoreType.DMA
    vmem = pltpu.VMEM
    args = (
        positions,
        masses.reshape(QUARTERS * TILES, LANES),
        centres.reshape(3 * HALOS // LANES, LANES),
        pair_halo,
        pair_tile,
        halo_slot,
        feedback,
        mixing,
        drive,
        readout,
    )
    share = (3 * TILES, LANES)
    return pl.pallas_call(
        kernel,
        out_shape=jax.ShapeDtypeStruct(positions.shape, F32),
        in_specs=[pl.BlockSpec(memory_space=pl.ANY)] * len(args),
        out_specs=pl.BlockSpec(memory_space=vmem),
        scratch_shapes=[
            *(vmem(a.shape, a.dtype) for a in args),
            dma((len(args),)),
            vmem((TILES, 4 * BLK), F32),
            vmem((4 * TILES, 4 * BLK), BF16),
            vmem((16, HALOS), F32),
            vmem((PAIRS, 4 * BLK), F32),
            vmem((PAIRS, LANES), F32),
            vmem((3, PAIRS, BLK), F32),
            vmem((PAIRS, BLK), jnp.int32),
            vmem((PAIRS, BLK), F32),
            vmem((2, 18 * 16, BLK), BF16),
            vmem((2, 256, BLK), BF16),
            vmem((2, 18 * 16, 256), F32),
            vmem((PAIRS, KNOTS), F32),
            vmem((2 * N_Z, PLANE, KNOTS), F32),
            vmem((N_Z, PLANE, KNOTS), F32),
            vmem((N_Z, PLANE, KNOTS), F32),
            vmem((STEPS, N_Y - 1, 2, OWNED, KNOTS), F32),
            vmem((DIRECT, N_Y - 1, 2, OWNED, KNOTS), F32),
            vmem((N_Z, OWNED, KNOTS), F32),
            vmem((N_Z - 1, OWNED, KNOTS), F32),
            vmem((3, 2 * KNOTS, 2 * KNOTS), BF16),
            vmem((2 * N_Z, PLANE, KNOTS), F32),
            vmem((2, PAIRS, ROWS), BF16),
            vmem((TILES, PAIRS), BF16),
            vmem((PAIRS, KNOTS), F32),
            vmem((PAIRS, 6 * LANES), BF16),
            vmem((N_X, *share), F32),
            vmem((N_X - 1, *share), F32),
            vmem(share, F32),
            vmem((N_X - 1, *share), F32),
            dma((STEPS,)),
            dma((STEPS,)),
            dma,
            dma((STEPS,)),
            dma,
            dma((DIRECT,)),
            dma,
            dma,
            dma,
            dma((len(TURNS),)),
            dma,
            dma((len(TURNS),)),
            dma,
            dma((len(TURNS) - PASSED,)),
            dma((len(TURNS),)),
            dma((len(TURNS),)),
            dma((PARTS, N_X - 1)),
            dma((PARTS, N_X - 1)),
            dma((PARTS, N_X - 1)),
            dma((PARTS, N_X - 1)),
        ],
        compiler_params=pltpu.CompilerParams(
            vmem_limit_bytes=VMEM_BYTES, collective_id=0, has_side_effects=True
        ),
    )(*args)


def solution(mesh):
    return jax.shard_map(
        per_device,
        mesh=mesh,
        in_specs=(
            P(None, "space"),
            P("space"),
            P("halo", None, None),
            P("halo", "space"),
            P("halo", "space"),
            P("halo", None),
            P("halo", "space"),
            P(),
            P(),
            P(),
        ),
        out_specs=P(None, "space"),
        check_vma=False,
    )
```

```python
import jax
import jax.numpy as jnp
from jax import lax
from jax.experimental import pallas as pl
from jax.experimental.pallas import tpu as pltpu
from jax.sharding import PartitionSpec as P

BLK = 512
ITERS = 8
KNOTS = 128
TILES = 32
PAIRS = 256
HALOS = 1024
OWNED = 16
N_Y = 4
N_Z = 8
N_X = 4
PLANE = N_Y * OWNED
ROWS = N_Z * PLANE
SUMS = ((0, 1), (1, 2), (3, 2), (5, 2), (7, 1))
STEPS = len(SUMS)
DIRECT = SUMS[0][1]
ORDER = (4, 3, 5, 2, 6, 1, 7, 0)
TURNS = ((7, 1), (6, 1), (4, 2), (2, 2), (0, 2))
TURNS_OF = (4, 4, 3, 3, 2, 2, 1)
PASSED = 3
LANES = 128
QUARTERS = BLK // LANES
PARTS = 2
PART = 3 * TILES // PARTS
VMEM_BYTES = 60 * 2**20
SCALE = (KNOTS - 1) / 2.6
F32 = jnp.float32
BF16 = jnp.bfloat16
MESH = pl.DeviceIdType.MESH


def two_parts(x):
    high = x.astype(BF16)
    return high, (x - high.astype(F32)).astype(BF16)


def three_parts(x):
    high = x.astype(BF16)
    rest = x - high.astype(F32)
    middle = rest.astype(BF16)
    return high, middle, (rest - middle.astype(F32)).astype(BF16)


def one_hot(mask):
    return jnp.where(mask, 1.0, 0.0).astype(BF16)


def matmul(a, b):
    return jnp.dot(a, b, preferred_element_type=F32)


def kernel(
    pos_in, mass_in, centre_in, halo_in, tile_in, slot_in, feedback_in, mixing_in, drive_in, readout_in,
    out,
    pos, mass, centre, halo, tile, slot, feedback, mixing, drive, readout, loaded,
    raw, parts, lookup, gathered, columns, offset, knot, fraction, left, right, product, pair_rows,
    dense, half_in, sums, y_in, y_other, z_sums, z_in, weights, table, picked, tile_of, coef_rows, moved, shares, share_in, total, total_in,
    half_send, half_recv, y_send, y_recv, other_send, other_recv, z_send, z_recv,
    coef_z_send, coef_z_recv, coef_y_send, coef_y_recv, coef_both_send, coef_both_recv, pass_send, pass_recv,
    share_send, share_recv, total_send, total_recv,
):
    inputs = (pos_in, mass_in, centre_in, halo_in, tile_in, slot_in, feedback_in, mixing_in, drive_in, readout_in)
    copies_in = [
        pltpu.make_async_copy(source, target, loaded.at[i])
        for i, (source, target) in enumerate(
            zip(inputs, (pos, mass, centre, halo, tile, slot, feedback, mixing, drive, readout))
        )
    ]
    for i in (5, 3, 4, 2, 0, 1, 6, 7, 8, 9):
        copies_in[i].start()

    me = lax.axis_index("space")
    x = lax.axis_index("halo")
    core, y, z = lax.rem(me, 2), lax.rem(lax.div(me, 2), N_Y), lax.div(me, 2 * N_Y)

    def at(dz=0, dy=0, other=0):
        place = lax.rem(z + dz + N_Z, N_Z) * N_Y + lax.rem(y + dy + N_Y, N_Y)
        return {"space": place * 2 + (1 - core if other else core)}

    def beside(d):
        return {"halo": lax.rem(x + d + N_X, N_X)}

    def send(source, target, send_sem, recv_sem, device):
        copy = pltpu.make_async_remote_copy(
            src_ref=source,
            dst_ref=target,
            send_sem=send_sem,
            recv_sem=recv_sem,
            device_id=device,
            device_id_type=MESH,
        )
        copy.start()
        return copy

    def wait_bytes(ref, sem):
        pltpu.make_async_copy(ref, ref, sem).wait()

    barrier = pltpu.get_barrier_semaphore()
    partners = [at(other=1)]
    partners += [at(dy=d, other=o) for d in range(1, N_Y) for o in range(2)]
    partners += [at(dz=d) for d in range(1, N_Z)]
    partners += [beside(d) for d in range(1, N_X)]
    for partner in partners:
        pl.semaphore_signal(barrier, inc=1, device_id=partner, device_id_type=MESH)

    for i in (2, 3, 4, 5):
        copies_in[i].wait()
    owner = lax.div(slot[...], OWNED)
    half = lax.rem(lax.rem(owner, 2) - core + 2, 2)
    far_y = lax.rem(lax.rem(lax.div(owner, 2), N_Y) - y + N_Y, N_Y)
    far_z = lax.rem(lax.div(owner, 2 * N_Y) - z + N_Z, N_Z)
    turn = jnp.where(far_z < N_Z // 2, N_Z - 1 - 2 * far_z, 2 * far_z - N_Z)
    row = half * ROWS + turn * PLANE + far_y * OWNED + lax.rem(slot[...], OWNED)
    lookup[...] = jnp.zeros_like(lookup)
    for j, part in enumerate(three_parts(centre[...])):
        part = part.astype(F32)
        for c in range(3):
            for i in range(HALOS // LANES):
                at_row = c * (HALOS // LANES) + i
                lookup[3 * j + c : 3 * j + c + 1, i * LANES : (i + 1) * LANES] = part[at_row : at_row + 1, :]
    lookup[9:10, :] = lax.div(row, 32).astype(F32)
    lookup[10:11, :] = lax.rem(row, 32).astype(F32)
    halo_is = one_hot(lax.broadcasted_iota(jnp.int32, (HALOS, PAIRS), 0) == halo[...])
    found = matmul(lookup[...].astype(BF16), halo_is)
    pair_row = found[9:10] * 32.0 + found[10:11]
    by_pair = jnp.concatenate(
        [
            found[0:3] + found[3:6] + found[6:9],
            pair_row,
            tile[...].astype(F32),
            jnp.zeros((LANES - 5, PAIRS), F32),
        ],
        axis=0,
    )
    columns[...] = by_pair.T

    for i in (0, 1):
        copies_in[i].wait()
    for t in range(TILES):
        for c in range(3):
            raw[t : t + 1, c * BLK : (c + 1) * BLK] = pos[c : c + 1, t * BLK : (t + 1) * BLK]
    for q in range(QUARTERS):
        raw[:, 3 * BLK + q * LANES : 3 * BLK + (q + 1) * LANES] = mass[pl.ds(q, TILES, stride=QUARTERS), :]
    for j, part in enumerate(three_parts(raw[...])):
        parts[j * TILES : (j + 1) * TILES, :] = part
    parts[3 * TILES :, :] = jnp.zeros((TILES, 4 * BLK), BF16)
    lane = lax.broadcasted_iota(jnp.int32, (PAIRS, LANES), 1)
    tile_is = one_hot((lax.rem(lane, TILES).astype(F32) == columns[:, 4:5]) & (lane < 3 * TILES))
    gathered[...] = matmul(tile_is, parts[...])

    lane8 = lax.broadcasted_iota(jnp.int32, (8, LANES), 1)
    sub8 = lax.broadcasted_iota(jnp.int32, (8, LANES), 0)
    low_lane = lax.rem(lane8, 16)

    def build(start, u):
        rows = pl.ds(pl.multiple_of(start, 16), 16)
        square = jnp.zeros((16, BLK), F32)
        for c in range(3):
            part = gathered[rows, c * BLK : (c + 1) * BLK] - columns[rows, c : c + 1]
            offset[c, rows, :] = part
            square += part * part
        scaled = jnp.sqrt(square) * SCALE
        below = jnp.floor(scaled)
        rest = scaled - below
        knot[rows, :] = below.astype(jnp.int32)
        fraction[rows, :] = rest
        coarse = jnp.floor(below * 0.125)
        fine = (below - 8.0 * coarse).astype(BF16)
        coarse = coarse.astype(BF16)
        weight = gathered[rows, 3 * BLK :]
        above = weight * rest
        w_below, w_above = two_parts(weight - above), two_parts(above)
        nothing, one = jnp.zeros((16, BLK), BF16), jnp.ones((16, BLK), BF16)
        masks = [fine == jnp.asarray(h, BF16) for h in range(8)]
        for j in range(2):
            for h in range(9):
                value = jnp.where(masks[h - 1], w_above[j], nothing) if h > 0 else nothing
                if h < 8:
                    value = jnp.where(masks[h], w_below[j], value)
                spot = (j * 9 + h) * 16
                left[u, spot : spot + 16, :] = value
        for j in range(16):
            number = (j % 8) * 2 + j // 8
            right[u, j * 16 : j * 16 + 16, :] = jnp.where(coarse == jnp.asarray(number, BF16), one, nothing)

    def fold(start, u):
        for e in range(2):
            source = (lane8 - low_lane) + sub8 + 8 * e
            profile = jnp.zeros((8, LANES), F32)
            for v in range(2):
                for h in range(9):
                    spot = h * 16 + 8 * e
                    both = (
                        product[u, spot : spot + 8, v * LANES : (v + 1) * LANES]
                        + product[u, 144 + spot : 144 + spot + 8, v * LANES : (v + 1) * LANES]
                    )
                    own = jnp.take_along_axis(both, source, axis=1)
                    to = 8 * v + h
                    if to == 16:
                        own = pltpu.roll(own, 16, 1)
                    profile += jnp.where(low_lane == to % 16, own, 0.0)
            pair_rows[pl.ds(pl.multiple_of(start + 8 * e, 8), 8), :] = profile

    def block(b, carry):
        for u in range(2):
            build(b * 32 + u * 16, u)
            product[u] = lax.dot_general(
                left[u], right[u], (((1,), (1,)), ((), ())), preferred_element_type=F32
            )
            fold(b * 32 + u * 16, u)
        return carry

    lax.fori_loop(0, PAIRS // 32, block, 0, unroll=8)

    profiles = jnp.concatenate(two_parts(pair_rows[...]), axis=1)

    def sum_rows(first, count):
        rows_of = lax.broadcasted_iota(jnp.int32, (count * PLANE, PAIRS), 0) + first * PLANE
        both = matmul(one_hot(rows_of == pair_row.astype(jnp.int32)), profiles)
        dense[first : first + count] = (both[:, :KNOTS] + both[:, KNOTS:]).reshape(count, PLANE, KNOTS)

    sum_rows(0, DIRECT)
    sum_rows(N_Z, DIRECT)

    pl.semaphore_wait(barrier, len(partners))
    for d in (2, 1, 3):
        rows = pl.ds(d * OWNED, OWNED)
        send(dense.at[pl.ds(0, DIRECT), rows], y_in.at[d - 1, pl.ds(0, DIRECT)], y_send, y_recv.at[0], at(dy=d))
        send(
            dense.at[pl.ds(N_Z, DIRECT), rows],
            y_other.at[d - 1],
            other_send,
            other_recv,
            at(dy=d, other=1),
        )
    sum_rows(N_Z + DIRECT, N_Z - DIRECT)
    halves = []
    for j, (first, count) in enumerate(SUMS):
        rows = pl.ds(0, PLANE if j else OWNED)
        halves.append(
            send(
                dense.at[pl.ds(N_Z + first, count), rows],
                half_in.at[pl.ds(first, count), rows],
                half_send.at[j],
                half_recv.at[j],
                at(other=1),
            )
        )
    sum_rows(DIRECT, N_Z - DIRECT)
    for i in (6, 7, 8, 9):
        copies_in[i].wait()
    for c in range(3):
        high, low = two_parts(mixing[c])
        weights[c, :KNOTS, :KNOTS] = high
        weights[c, KNOTS:, :KNOTS] = high
        weights[c, :KNOTS, KNOTS:] = low
        weights[c, KNOTS:, KNOTS:] = low
    eye = lax.broadcasted_iota(jnp.int32, (OWNED, OWNED), 0) == lax.broadcasted_iota(
        jnp.int32, (OWNED, OWNED), 1
    )
    phi = jnp.sum(jnp.where(eye, feedback[...], 0.0), axis=1, keepdims=True)

    rows_of = lax.broadcasted_iota(jnp.int32, (PAIRS, ROWS), 1).astype(F32)
    for first in range(2):
        picked[first] = one_hot(rows_of + first * float(ROWS) == columns[:, 3:4])
    tile_of[...] = one_hot(lax.broadcasted_iota(jnp.int32, (TILES, PAIRS), 0) == tile[...])

    for j, (first, count) in enumerate(SUMS[1:], 1):
        halves[j].wait_recv()
        turns = pl.ds(first, count)
        sums[turns] = dense[turns] + half_in[turns]
        for d in (2, 1, 3):
            send(
                sums.at[turns, pl.ds(d * OWNED, OWNED)],
                y_in.at[d - 1, turns],
                y_send,
                y_recv.at[j],
                at(dy=d),
            )
    for j, (first, count) in enumerate(SUMS):
        turns = slice(first, first + count)
        if j == 0:
            halves[j].wait_recv()
            wait_bytes(y_other, other_recv)
            plane = dense[turns, :OWNED] + half_in[turns, :OWNED] + y_other[0] + y_other[1] + y_other[2]
        else:
            plane = sums[turns, :OWNED]
        wait_bytes(y_in.at[pl.ds(0, N_Y - 1), pl.ds(first, count)], y_recv.at[j])
        plane += y_in[0, turns] + y_in[1, turns] + y_in[2, turns]
        z_sums[turns] = plane
        for i in range(first, first + count):
            if ORDER[i]:
                send(z_sums.at[i], z_in.at[i], z_send, z_recv, at(dz=ORDER[i]))
    wait_bytes(z_in, z_recv)
    owned = z_sums[N_Z - 1]
    for i in range(N_Z - 1):
        owned += z_in[i]

    level = jnp.log1p(owned)
    driven = [drive[c : c + 1, :] * level for c in range(3)]
    state = [jnp.tanh(v) for v in driven]
    for _ in range(ITERS - 1):
        mean = (state[0] + state[1] + state[2]) * (0.5 / 3.0)
        fresh = []
        for c in range(3):
            mixed = matmul(jnp.concatenate(two_parts(state[c]), axis=1), weights[c])
            mixed = mixed[:, :KNOTS] + mixed[:, KNOTS:]
            fresh.append(jnp.tanh(driven[c] + phi * mixed + mean))
        state = fresh
    table[N_Z - 1, :OWNED] = (
        readout[0:1, :] * state[0] + readout[1:2, :] * state[1] + readout[2:3, :] * state[2]
    )

    own = table.at[N_Z - 1, pl.ds(0, OWNED)]
    for i in range(N_Z - 1):
        send(own, table.at[i, pl.ds(0, OWNED)], coef_z_send, coef_z_recv.at[TURNS_OF[i]], at(dz=-ORDER[i]))
    passed = []
    for g, (first, count) in enumerate(TURNS):
        line = table.at[pl.ds(first, count), pl.ds(0, OWNED)]
        if g > 0:
            wait_bytes(line, coef_z_recv.at[g])
        for d in (2, 1, 3):
            send(
                line,
                table.at[pl.ds(first, count), pl.ds(d * OWNED, OWNED)],
                coef_y_send,
                coef_y_recv.at[g],
                at(dy=-d),
            )
        if g >= PASSED:
            for d in (2, 1, 3):
                send(
                    line,
                    table.at[pl.ds(N_Z + first, count), pl.ds(d * OWNED, OWNED)],
                    coef_both_send,
                    coef_both_recv.at[g - PASSED],
                    at(dy=-d, other=1),
                )
            passed.append(
                send(
                    line,
                    table.at[pl.ds(N_Z + first, count), pl.ds(0, OWNED)],
                    pass_send.at[g],
                    pass_recv.at[g],
                    at(other=1),
                )
            )
    for g, (first, count) in enumerate(TURNS):
        wait_bytes(table.at[pl.ds(first, count), pl.ds(OWNED, 3 * OWNED)], coef_y_recv.at[g])
        if g < PASSED:
            passed.append(
                send(
                    table.at[pl.ds(first, count)],
                    table.at[pl.ds(N_Z + first, count)],
                    pass_send.at[g],
                    pass_recv.at[g],
                    at(other=1),
                )
            )

    def coefficients(first):
        rows = table[first * N_Z : (first + 1) * N_Z].reshape(ROWS, KNOTS)
        both = matmul(picked[first], jnp.concatenate(two_parts(rows), axis=1))
        return both[:, :KNOTS] + both[:, KNOTS:]

    coef_rows[...] = coefficients(0)
    for copy in passed:
        copy.wait_recv()
    for g, (first, count) in enumerate(TURNS[PASSED:]):
        wait_bytes(table.at[pl.ds(N_Z + first, count), pl.ds(OWNED, 3 * OWNED)], coef_both_recv.at[g])
    coef_rows[...] += coefficients(1)

    combined = []
    for d in (2, 1, 3, 0):
        lanes = pl.ds(pl.multiple_of(lax.rem(x + d, N_X) * LANES, LANES), LANES)

        def evaluate(b, carry):
            rows = pl.ds(pl.multiple_of(b * 16, 16), 16)
            coef = coef_rows[rows, :]
            step = pltpu.roll(coef, KNOTS - 1, 1) - coef
            index = knot[rows, lanes]
            scalar = jnp.take_along_axis(coef, index, axis=1) + fraction[
                rows, lanes
            ] * jnp.take_along_axis(step, index, axis=1)
            for c in range(3):
                high, low = two_parts(offset[c, rows, lanes] * scalar)
                moved[rows, c * LANES : (c + 1) * LANES] = high
                moved[rows, (c + 3) * LANES : (c + 4) * LANES] = low
            return carry

        lax.fori_loop(0, PAIRS // 16, evaluate, 0, unroll=16)
        share = matmul(tile_of[...], moved[...])
        for c in range(3):
            shares[d, c * TILES : (c + 1) * TILES, :] = (
                share[:, c * LANES : (c + 1) * LANES] + share[:, (c + 3) * LANES : (c + 4) * LANES]
            )
        if d > 0:
            for part in range(PARTS):
                rows = pl.ds(part * PART, PART)
                combined.append(
                    send(
                        shares.at[d, rows],
                        share_in.at[d - 1, rows],
                        share_send.at[part, d - 1],
                        share_recv.at[part, d - 1],
                        beside(d),
                    )
                )
    finished = []
    for part in range(PARTS):
        for copy in combined[part::PARTS]:
            copy.wait_recv()
        rows = pl.ds(part * PART, PART)
        total[rows, :] = shares[0, rows] + share_in[0, rows] + share_in[1, rows] + share_in[2, rows]
        for d in (2, 1, 3):
            finished.append(
                send(
                    total.at[rows],
                    total_in.at[d - 1, rows],
                    total_send.at[part, d - 1],
                    total_recv.at[part, d - 1],
                    beside(-d),
                )
            )

    def lay_out(part, quarter):
        for t in range(TILES):
            lanes = pl.ds(pl.multiple_of(t * BLK + quarter * LANES, LANES), LANES)
            for c in range(3):
                out[c : c + 1, lanes] = part[c * TILES + t : c * TILES + t + 1, :]

    lay_out(total, x)
    for i, d in ((1, 1), (2, 3), (0, 2)):
        for part in range(PARTS):
            finished[3 * part + i].wait_recv()
        lay_out(total_in.at[d - 1], lax.rem(x + d, N_X))
    for copy in (*halves, *passed, *combined, *finished):
        copy.wait_send()
    wait_bytes(y_in, y_send)
    wait_bytes(y_other, other_send)
    wait_bytes(y_in, coef_y_send)
    wait_bytes(table.at[pl.ds(0, 4), pl.ds(OWNED, 3 * OWNED)], coef_both_send)
    wait_bytes(z_in, z_send)
    wait_bytes(z_in, coef_z_send)


def per_device(
    positions, masses, centres, pair_halo, pair_tile, halo_slot, feedback, mixing, drive, readout
):
    dma = pltpu.SemaphoreType.DMA
    vmem = pltpu.VMEM
    args = (
        positions,
        masses.reshape(QUARTERS * TILES, LANES),
        centres.reshape(3 * HALOS // LANES, LANES),
        pair_halo,
        pair_tile,
        halo_slot,
        feedback,
        mixing,
        drive,
        readout,
    )
    share = (3 * TILES, LANES)
    return pl.pallas_call(
        kernel,
        out_shape=jax.ShapeDtypeStruct(positions.shape, F32),
        in_specs=[pl.BlockSpec(memory_space=pl.ANY)] * len(args),
        out_specs=pl.BlockSpec(memory_space=vmem),
        scratch_shapes=[
            *(vmem(a.shape, a.dtype) for a in args),
            dma((len(args),)),
            vmem((TILES, 4 * BLK), F32),
            vmem((4 * TILES, 4 * BLK), BF16),
            vmem((16, HALOS), F32),
            vmem((PAIRS, 4 * BLK), F32),
            vmem((PAIRS, LANES), F32),
            vmem((3, PAIRS, BLK), F32),
            vmem((PAIRS, BLK), jnp.int32),
            vmem((PAIRS, BLK), F32),
            vmem((2, 18 * 16, BLK), BF16),
            vmem((2, 256, BLK), BF16),
            vmem((2, 18 * 16, 256), F32),
            vmem((PAIRS, KNOTS), F32),
            vmem((2 * N_Z, PLANE, KNOTS), F32),
            vmem((N_Z, PLANE, KNOTS), F32),
            vmem((N_Z, PLANE, KNOTS), F32),
            vmem((N_Y - 1, N_Z, OWNED, KNOTS), F32),
            vmem((N_Y - 1, DIRECT, OWNED, KNOTS), F32),
            vmem((N_Z, OWNED, KNOTS), F32),
            vmem((N_Z - 1, OWNED, KNOTS), F32),
            vmem((3, 2 * KNOTS, 2 * KNOTS), BF16),
            vmem((2 * N_Z, PLANE, KNOTS), F32),
            vmem((2, PAIRS, ROWS), BF16),
            vmem((TILES, PAIRS), BF16),
            vmem((PAIRS, KNOTS), F32),
            vmem((PAIRS, 6 * LANES), BF16),
            vmem((N_X, *share), F32),
            vmem((N_X - 1, *share), F32),
            vmem(share, F32),
            vmem((N_X - 1, *share), F32),
            dma((STEPS,)),
            dma((STEPS,)),
            dma,
            dma((STEPS,)),
            dma,
            dma,
            dma,
            dma,
            dma,
            dma((len(TURNS),)),
            dma,
            dma((len(TURNS),)),
            dma,
            dma((len(TURNS) - PASSED,)),
            dma((len(TURNS),)),
            dma((len(TURNS),)),
            dma((PARTS, N_X - 1)),
            dma((PARTS, N_X - 1)),
            dma((PARTS, N_X - 1)),
            dma((PARTS, N_X - 1)),
        ],
        compiler_params=pltpu.CompilerParams(
            vmem_limit_bytes=VMEM_BYTES, collective_id=0, has_side_effects=True
        ),
    )(*args)


def solution(mesh):
    return jax.shard_map(
        per_device,
        mesh=mesh,
        in_specs=(
            P(None, "space"),
            P("space"),
            P("halo", None, None),
            P("halo", "space"),
            P("halo", "space"),
            P("halo", None),
            P("halo", "space"),
            P(),
            P(),
            P(),
        ),
        out_specs=P(None, "space"),
        check_vma=False,
    )
```
